32 devices in a mesh: groups: 2 (over x), bunch: 8 (over z, y), pencil: 2 (over core).
Axes of the slice: x: 2, y: 2, z: 4, core: 2. Of those that a mesh axis runs over, the one named last changes fastest.
Arguments:
- charge: bfloat16 [16, 32768], P(('groups', 'bunch'), 'pencil'), parts along dimension 0, may hold values from 0.25 to 4
- cell_deposit: int32 [16, 32768], P(('groups', 'bunch'), 'pencil'), parts along dimension 0, may hold values from 0 to 65535
- cell_gather: int32 [16, 32768], P(('groups', 'bunch'), 'pencil'), parts along dimension 0, may hold values from 0 to 65535
- green_spectra: float32 [7, 2, 64, 64, 128], P(None, None, None, 'pencil'), may hold values from -6 to 6
Outputs:
- field_at_particles: float32 [3, 16, 32768], P(None, ('groups', 'bunch'), 'pencil'), parts along dimension 1
The draws below stay inside these ranges and needn't reach their ends.
There are 2 independent parts, one for each index of `groups`. The reference program is written for one: setup_inputs(seed, part) draws one part's arguments, and reference() takes and returns one part's arrays. A program takes and returns all parts, laid end to end along the dimension named above; an argument that names none is the same for every part. Nothing has to cross between parts.
Inputs may be any that keep to these rules, and one draw needn't show every extreme that they name: `cell_deposit`: flat cell index (x * 32 + y) * 64 + z. `cell_gather`: flat cell index (x * 32 + y) * 64 + z.
All inputs are finite; a program needn't handle non-finite values.
Results may differ from the reference program's by a relative error of at most 0.0029.
Values may be sent and summed in bfloat16 or wider, within the bound.
No kernel may reach another device: no remote copies, remote signals or barrier semaphores. Data moves between devices by JAX's collectives and lax.ppermute only.
A program may use at most 128 MiB of HBM per device.

```python
import math
import jax
import jax.numpy as jnp
from jax import lax

GX = 32
GY = 32
GZ = 64
SPAN = 3
MX = 64
MY = 64
MZ = 128
OFFSETS = 7
BUNCHES = 8
PARTICLES = 32768


def set_ends(entries, rng, low, top_value):
    longest = entries.shape.index(max(entries.shape))
    spots = []
    for shift in (0, 1):
        where = [jax.random.randint(jax.random.fold_in(rng, axis), (), 0, length) for axis, length in enumerate(entries.shape)]
        where[longest] = (where[longest] + shift) % entries.shape[longest]
        spots.append(tuple(where))
    return entries.at[spots[0]].set(low).at[spots[1]].set(top_value)


def steps_of(own_key, shape, split, least, high):
    gain, own = 1.0, jax.random.fold_in(own_key, 6)
    for axis_at, blocks in split:
        steps = jnp.exp(jax.random.uniform(jax.random.fold_in(own, axis_at), (blocks,), jnp.float32, least / len(split), high / len(split)))
        gain = gain * jnp.repeat(steps, shape[axis_at] // blocks).reshape([-1 if axis == axis_at else 1 for axis in range(len(shape))])
    return gain


def noise(stream_key, shape, deviation, most, shards=(), kind=jnp.bfloat16):
    loudness = steps_of(stream_key, shape, shards, -0.22, 0.18) if shards else 1.0
    array = jax.random.normal(stream_key, shape, jnp.float32) * deviation * loudness
    return jnp.minimum(jnp.maximum(array, -most), most).astype(kind)


def setup_inputs(seed: int = 0, part: int = 0) -> dict:
    seeds = jax.random.split(jax.random.key(seed), 5)
    part_keys = jax.random.split(jax.random.fold_in(seeds[4], part), 5)
    return {
        "charge": jnp.clip(jnp.exp(math.log(4.0) - 2.7725887 * jax.random.uniform(part_keys[0], (BUNCHES, PARTICLES), jnp.float32) ** steps_of(part_keys[0], (BUNCHES, PARTICLES), ((0, 8), (1, 2)), -0.2, 0.2)), 0.25, 4.0).astype(jnp.bfloat16),
        "cell_deposit": set_ends(jax.random.randint(part_keys[1], (BUNCHES, PARTICLES), 0, GX * GY * GZ), jax.random.fold_in(part_keys[1], 1), 0, (GX * GY * GZ) - 1).astype(jnp.int32),
        "cell_gather": set_ends(jax.random.randint(part_keys[2], (BUNCHES, PARTICLES), 0, GX * GY * GZ), jax.random.fold_in(part_keys[2], 1), 0, (GX * GY * GZ) - 1).astype(jnp.int32),
        "green_spectra": noise(seeds[3], (OFFSETS, 2, MX, MY, MZ), 1.0, 6.0, ((3, 2),), jnp.float32),
    }


def spectrum_of(bunch_charge, bunch_cells):
    density = jax.ops.segment_sum(bunch_charge.astype(jnp.float32), bunch_cells, num_segments=GX * GY * GZ)
    density = density.reshape(GX, GY, GZ)
    return jnp.fft.fftn(density, s=(MX, MY, MZ))


def reference(charge, cell_deposit, cell_gather, green_spectra):
    spectra = lax.map(lambda paired: spectrum_of(paired[0], paired[1]), (charge, cell_deposit))
    green = lax.complex(green_spectra[:, 0], green_spectra[:, 1])
    padding = jnp.zeros((SPAN, MX, MY, MZ), spectra.dtype)
    padded = jnp.concatenate([padding, spectra, padding], axis=0)
    total = jnp.zeros_like(spectra)
    for offset in range(-SPAN, SPAN + 1):
        shifted = padded[SPAN - offset:SPAN - offset + BUNCHES]
        total = total + green[offset + SPAN][None] * shifted
    potential = jnp.real(jnp.fft.ifftn(total, axes=(1, 2, 3)))[:, :GX, :GY, :GZ]
    beside_all = jnp.pad(potential, ((0, 0), (1, 1), (1, 1), (1, 1)))
    field_x = 0.5 * (beside_all[:, :-2, 1:-1, 1:-1] - beside_all[:, 2:, 1:-1, 1:-1])
    field_y = 0.5 * (beside_all[:, 1:-1, :-2, 1:-1] - beside_all[:, 1:-1, 2:, 1:-1])
    field_z = 0.5 * (beside_all[:, 1:-1, 1:-1, :-2] - beside_all[:, 1:-1, 1:-1, 2:])
    field = jnp.stack([field_x, field_y, field_z], axis=1).astype(jnp.bfloat16)
    flat_field = field.reshape(BUNCHES, 3, GX * GY * GZ).astype(jnp.float32)
    picked = jnp.take_along_axis(flat_field, cell_gather[:, None, :].astype(jnp.int32), axis=2)
    return jnp.transpose(picked, (1, 0, 2))
```

```python
import functools

import jax
import jax.numpy as jnp
import numpy as np
from jax import lax
from jax.experimental import pallas as pl
from jax.experimental.pallas import tpu as pltpu
from jax.sharding import PartitionSpec as P

GX = 32
GY = 32
GZ = 64
SPAN = 3
MX = 64
MY = 64
MZ = 128
BF16 = jnp.bfloat16
F32 = jnp.float32
DEPOSIT_BLOCK = 2048
GATHER_BLOCK = 1024


def hi_lo(table):
    top = table.astype(np.float32).astype(BF16)
    rest = (table - top.astype(np.float64)).astype(np.float32).astype(BF16)
    return top, rest


def stacked_terms(table):
    top, rest = hi_lo(table)
    return np.concatenate([top, top, rest], axis=-1)


def phases(rows, columns, period):
    angles = 2.0 * np.pi / period * ((rows[:, None] * columns[None, :]) % period)
    return np.cos(angles), np.sin(angles)


def make_tables(pencils):
    width = MY // pencils
    cos_z, sin_z = phases(np.arange(GZ), np.arange(MZ), MZ)
    piece = np.concatenate([cos_z, -sin_z], axis=1)
    forward_z = np.kron(np.eye(4), piece)
    grid_x = (np.arange(8)[None, :] * 4 + np.arange(4)[:, None]).reshape(-1)
    cos_x, sin_x = phases(np.arange(MX), grid_x, MX)
    forward_x = np.block([[cos_x, sin_x], [-sin_x, cos_x]])
    forward_y = []
    inverse_y = []
    for pencil in range(pencils):
        own = np.arange(pencil * width, (pencil + 1) * width)
        cos_y, sin_y = phases(own, np.arange(GY), MY)
        forward_y.append(stacked_terms(np.block([[cos_y, sin_y], [-sin_y, cos_y]])))
        inverse_y.append(stacked_terms(np.concatenate([cos_y.T, sin_y.T], axis=0)))
    cos_b, sin_b = phases(np.arange(MZ), np.arange(GZ), MZ)
    inverse_z = np.block([[cos_b, sin_b], [-sin_b, cos_b]])
    cos_c, sin_c = phases(np.arange(GX), np.arange(MX), MX)
    inverse_x = np.concatenate([cos_c, sin_c], axis=0) / float(MX * MY * MZ)
    forward_hi, forward_lo = hi_lo(forward_z)
    inverse_hi, inverse_lo = hi_lo(inverse_z)
    return dict(
        z_hi=forward_hi,
        z_lo=forward_lo,
        x=stacked_terms(forward_x),
        y=np.stack(forward_y),
        iz_hi=inverse_hi,
        iz_lo=inverse_lo,
        iy=np.stack(inverse_y),
        ix=stacked_terms(inverse_x),
    )


def dot(a, b):
    return jnp.dot(a, b, preferred_element_type=F32)


def split(value):
    top = value.astype(BF16)
    return top, (value - top.astype(F32)).astype(BF16)


def data_terms(value):
    top, rest = split(value)
    return jnp.concatenate([top, rest, top], axis=0)


def deposit_kernel(cell_ref, charge_ref, out_ref):
    cell = cell_ref[...]
    row = ((cell >> 6) & 31) * 8 + (cell >> 13)
    column = ((cell >> 11) & 3) * 64 + (cell & 63)
    index = lax.broadcasted_iota(jnp.int32, (256, cell.shape[1]), 0)
    rows = (index == row).astype(F32).astype(BF16)
    weights = charge_ref[...].astype(F32)
    columns = jnp.where(index == column, weights, 0.0).astype(BF16)
    part = lax.dot_general(
        rows, columns, (((1,), (1,)), ((), ())), preferred_element_type=F32
    )

    @pl.when(pl.program_id(0) == 0)
    def _():
        out_ref[...] = part

    @pl.when(pl.program_id(0) > 0)
    def _():
        out_ref[...] += part


def deposit(cells, charge):
    count = cells.shape[1]
    block = min(DEPOSIT_BLOCK, count)
    return pl.pallas_call(
        deposit_kernel,
        grid=(count // block,),
        in_specs=[
            pl.BlockSpec((1, block), lambda i: (0, i)),
            pl.BlockSpec((1, block), lambda i: (0, i)),
        ],
        out_specs=pl.BlockSpec((256, 256), lambda i: (0, 0)),
        out_shape=jax.ShapeDtypeStruct((256, 256), F32),
        compiler_params=pltpu.CompilerParams(vmem_limit_bytes=32 * 2**20),
        name="deposit",
    )(cells, charge)


def spectral_kernel(
    order_ref,
    density_ref,
    green_ref,
    z_hi_ref,
    z_lo_ref,
    x_ref,
    y_ref,
    iz_hi_ref,
    iz_lo_ref,
    iy_ref,
    ix_ref,
    out_ref,
    after_z,
    after_x,
    total,
    back,
):
    step = pl.program_id(0)
    top, rest = split(density_ref[0])
    after_z[...] = dot(top, z_hi_ref[...]) + (
        dot(rest, z_hi_ref[...]) + dot(top, z_lo_ref[...])
    )
    for pair in range(GY // 2):
        sides = []
        for y in (2 * pair, 2 * pair + 1):
            tiles = [
                after_z[8 * y : 8 * y + 8, (2 * low + part) * MZ : (2 * low + part + 1) * MZ]
                for part in range(2)
                for low in range(4)
            ]
            sides.append(jnp.concatenate(tiles, axis=0))
        out = dot(x_ref[...], data_terms(jnp.concatenate(sides, axis=1)))
        after_x[4 * MZ * pair // 2 : 4 * MZ * pair // 2 + 128, :] = out[:, :MZ]
        after_x[4 * MZ * pair // 2 + 128 : 4 * MZ * pair // 2 + 256, :] = out[:, MZ:]

    @pl.when(step == 0)
    def _():
        total[...] = jnp.zeros_like(total)

    width = green_ref.shape[3]
    for pair in range(MX // 2):
        sides = []
        for kx in (2 * pair, 2 * pair + 1):
            real = after_x[pl.ds(kx, GY, stride=2 * MX), :]
            imag = after_x[pl.ds(MX + kx, GY, stride=2 * MX), :]
            sides.append(jnp.concatenate([real, imag], axis=0))
        out = dot(y_ref[0], data_terms(jnp.concatenate(sides, axis=1)))
        for side in range(2):
            kx = 2 * pair + side
            real = out[:width, side * MZ : (side + 1) * MZ]
            imag = out[width:, side * MZ : (side + 1) * MZ]
            green_real = green_ref[0, 0, kx]
            green_imag = green_ref[0, 1, kx]
            rows = pl.ds(kx * width, width)
            total[rows, :MZ] += green_real * real - green_imag * imag
            total[rows, MZ:] += green_real * imag + green_imag * real

    @pl.when(step == pl.num_programs(0) - 1)
    def _():
        lane = lax.broadcasted_iota(jnp.int32, (GY, 2 * GZ), 1)
        first = lane < GZ
        for group in range(MX // 8):
            top, rest = split(total[group * 8 * width : (group + 1) * 8 * width, :])
            turned = dot(top, iz_hi_ref[...]) + (
                dot(rest, iz_hi_ref[...]) + dot(top, iz_lo_ref[...])
            )
            for pair in range(4):
                sides = [
                    turned[(2 * pair + side) * width : (2 * pair + side + 1) * width, :]
                    for side in range(2)
                ]
                out = dot(iy_ref[0], data_terms(jnp.concatenate(sides, axis=1)))
                for side in range(2):
                    kx = group * 8 + 2 * pair + side
                    by_cos = out[:GY, side * MZ : (side + 1) * MZ]
                    by_sin = pltpu.roll(out[GY:, side * MZ : (side + 1) * MZ], GZ, 1)
                    back[kx * GY : (kx + 1) * GY, :] = by_cos + jnp.where(
                        first, -by_sin, by_sin
                    )
        for pair in range(GY // 2):
            sides = [back[pl.ds(2 * pair + side, MX, stride=GY), :] for side in range(2)]
            out = dot(ix_ref[...], data_terms(jnp.concatenate(sides, axis=1)))
            even = out[:GX, :MZ] - pltpu.roll(out[GX:, :MZ], GZ, 1)
            odd = pltpu.roll(out[:GX, MZ:], GZ, 1) - out[GX:, MZ:]
            out_ref[pair * GX : (pair + 1) * GX, :] = jnp.where(first, even, odd)


def spectral(order, densities, green, tables):
    offsets, _, _, width, _ = green.shape

    def whole(table):
        return pl.BlockSpec(table.shape, lambda i, order: (0,) * table.ndim)

    def by_pencil(table):
        return pl.BlockSpec((1,) + table.shape[1:], lambda i, order: (order[offsets], 0, 0))

    return pl.pallas_call(
        spectral_kernel,
        grid_spec=pltpu.PrefetchScalarGridSpec(
            num_scalar_prefetch=1,
            grid=(offsets,),
            in_specs=[
                pl.BlockSpec((1, 256, 256), lambda i, order: (i, 0, 0)),
                pl.BlockSpec((1, 2, MX, width, MZ), lambda i, order: (order[i], 0, 0, 0, 0)),
                whole(tables["z_hi"]),
                whole(tables["z_lo"]),
                whole(tables["x"]),
                by_pencil(tables["y"]),
                whole(tables["iz_hi"]),
                whole(tables["iz_lo"]),
                by_pencil(tables["iy"]),
                whole(tables["ix"]),
            ],
            out_specs=pl.BlockSpec((512, 128), lambda i, order: (0, 0)),
            scratch_shapes=[
                pltpu.VMEM((256, 1024), F32),
                pltpu.VMEM((GY * 2 * MX, MZ), F32),
                pltpu.VMEM((MX * width, 2 * MZ), F32),
                pltpu.VMEM((MX * GY, 2 * GZ), F32),
            ],
        ),
        out_shape=jax.ShapeDtypeStruct((512, 128), F32),
        compiler_params=pltpu.CompilerParams(vmem_limit_bytes=48 * 2**20),
        name="spectral",
    )(
        order,
        densities,
        green,
        *(tables[name] for name in ("z_hi", "z_lo", "x", "y", "iz_hi", "iz_lo", "iy", "ix")),
    )


def gather_kernel(own_ref, other_ref, cell_ref, out_ref, field):
    @pl.when(pl.program_id(0) == 0)
    def _():
        potential = own_ref[...] + other_ref[...]
        lane = lax.broadcasted_iota(jnp.int32, (512, 128), 1)
        row = lax.broadcasted_iota(jnp.int32, (512, 128), 0)
        x = row % GX
        z = lane % GZ
        zero = jnp.zeros((GX, 128), F32)
        below = jnp.where(x == 0, 0.0, pltpu.roll(potential, 1, 0))
        above = jnp.where(x == GX - 1, 0.0, pltpu.roll(potential, 511, 0))
        field_x = 0.5 * (below - above)
        turned = pltpu.roll(potential, GZ, 1)
        before = jnp.concatenate([zero, turned[: 512 - GX]], axis=0)
        after = jnp.concatenate([turned[GX:], zero], axis=0)
        field_y = 0.5 * (
            jnp.where(lane < GZ, before, turned) - jnp.where(lane < GZ, turned, after)
        )
        left = jnp.where(z == 0, 0.0, pltpu.roll(potential, 1, 1))
        right = jnp.where(z == GZ - 1, 0.0, pltpu.roll(potential, 127, 1))
        field_z = 0.5 * (left - right)
        for part, value in enumerate((field_x, field_y, field_z)):
            field[part * 128 : (part + 1) * 128, :] = jnp.transpose(value).astype(BF16)

    cell = cell_ref[...]
    y = (cell >> 6) & 31
    high = (y >> 1) * GX + (cell >> 11)
    low = (y & 1) * GZ + (cell & 63)
    count = cell.shape[1]
    index = lax.broadcasted_iota(jnp.int32, (512, count), 0)
    chosen = (index == high).astype(F32).astype(BF16)
    picked = dot(field[...], chosen)
    inside = index[:128] == low
    for part in range(3):
        values = jnp.where(inside, picked[part * 128 : (part + 1) * 128], 0.0)
        out_ref[part, :, :] = jnp.sum(values, axis=0, keepdims=True)


def gather(own, other, cells):
    count = cells.shape[1]
    block = min(GATHER_BLOCK, count)
    return pl.pallas_call(
        gather_kernel,
        grid=(count // block,),
        in_specs=[
            pl.BlockSpec((512, 128), lambda i: (0, 0)),
            pl.BlockSpec((512, 128), lambda i: (0, 0)),
            pl.BlockSpec((1, block), lambda i: (0, i)),
        ],
        out_specs=pl.BlockSpec((3, 1, block), lambda i: (0, 0, i)),
        out_shape=jax.ShapeDtypeStruct((3, 1, count), F32),
        scratch_shapes=[pltpu.VMEM((384, 512), BF16)],
        compiler_params=pltpu.CompilerParams(vmem_limit_bytes=32 * 2**20),
        name="gather",
    )(own, other, cells)


def per_device(tables, charge, cell_deposit, cell_gather, green_spectra):
    pencils = lax.axis_size("pencil")
    bunches = lax.axis_size("bunch")
    pencil = lax.axis_index("pencil")
    swap = [(i, (i + 1) % pencils) for i in range(pencils)]
    part = deposit(cell_deposit, charge)
    density = part + lax.ppermute(part, "pencil", swap)
    near = []
    for distance in range(1, SPAN + 1):
        route = []
        for bunch in range(bunches):
            for core, source in ((0, bunch - distance), (1, bunch + distance)):
                if 0 <= source < bunches:
                    route.append((source * pencils + core, bunch * pencils + core))
        near.append(lax.ppermute(density, ("bunch", "pencil"), route))
    near = jnp.stack(near)
    far = lax.ppermute(near, "pencil", swap)
    densities = jnp.concatenate([density[None], near, far], axis=0)
    steps = np.arange(1, SPAN + 1)
    up = np.concatenate([[SPAN], SPAN + steps, SPAN - steps, [0]])
    down = np.concatenate([[SPAN], SPAN - steps, SPAN + steps, [1]])
    order = jnp.where(pencil == 0, jnp.asarray(up, jnp.int32), jnp.asarray(down, jnp.int32))
    own = spectral(order, densities, green_spectra, tables)
    other = lax.ppermute(own, "pencil", swap)
    return gather(own, other, cell_gather)


def solution(mesh):
    in_specs = (
        P(("groups", "bunch"), "pencil"),
        P(("groups", "bunch"), "pencil"),
        P(("groups", "bunch"), "pencil"),
        P(None, None, None, "pencil", None),
    )
    out_specs = P(None, ("groups", "bunch"), "pencil")
    tables = make_tables(mesh.shape["pencil"])
    return jax.shard_map(
        functools.partial(per_device, tables),
        mesh=mesh,
        in_specs=in_specs,
        out_specs=out_specs,
        check_vma=False,
    )
```

```python
import functools

import jax
import jax.numpy as jnp
import numpy as np
from jax import lax
from jax.experimental import pallas as pl
from jax.experimental.pallas import tpu as pltpu
from jax.sharding import PartitionSpec as P

GX = 32
GY = 32
GZ = 64
SPAN = 3
MX = 64
MY = 64
MZ = 128
BF16 = jnp.bfloat16
F32 = jnp.float32
GATHER_CHUNK = 512
PITCH_X = 2 * MX + 1
PITCH_Y = GY + 1


def hi_lo(table):
    top = table.astype(np.float32).astype(BF16)
    rest = (table - top.astype(np.float64)).astype(np.float32).astype(BF16)
    return top, rest


def stacked_terms(table):
    top, rest = hi_lo(table)
    return np.concatenate([top, top, rest], axis=-1)


def phases(rows, columns, period):
    angles = 2.0 * np.pi / period * ((rows[:, None] * columns[None, :]) % period)
    return np.cos(angles), np.sin(angles)


def make_tables(pencils):
    width = MY // pencils
    cos_z, sin_z = phases(np.arange(GZ), np.arange(MZ), MZ)
    forward_z = np.concatenate([cos_z, -sin_z], axis=1)
    grid_x = (np.arange(8)[None, :] * 4 + np.arange(4)[:, None]).reshape(-1)
    cos_x, sin_x = phases(np.arange(MX), grid_x, MX)
    forward_x = np.block([[cos_x, sin_x], [-sin_x, cos_x]])
    forward_y = []
    inverse_y = []
    for pencil in range(pencils):
        own = np.arange(pencil * width, (pencil + 1) * width)
        cos_y, sin_y = phases(own, np.arange(GY), MY)
        forward_y.append(stacked_terms(np.block([[cos_y, sin_y], [-sin_y, cos_y]])))
        inverse_y.append(stacked_terms(np.concatenate([cos_y.T, sin_y.T], axis=0)))
    cos_b, sin_b = phases(np.arange(MZ), np.arange(GZ), MZ)
    inverse_z = np.block([[cos_b, sin_b], [-sin_b, cos_b]])
    cos_c, sin_c = phases(np.arange(GX), np.arange(MX), MX)
    inverse_x = np.concatenate([cos_c, sin_c], axis=0) / float(MX * MY * MZ)
    inverse_hi, inverse_lo = hi_lo(inverse_z)
    return dict(
        z=stacked_terms(forward_z.T).T,
        x=stacked_terms(forward_x),
        y=np.stack(forward_y),
        iz_hi=inverse_hi,
        iz_lo=inverse_lo,
        iy=np.stack(inverse_y),
        ix=stacked_terms(inverse_x),
    )


def dot(a, b):
    return jnp.dot(a, b, preferred_element_type=F32)


def split(value):
    top = value.astype(BF16)
    return top, (value - top.astype(F32)).astype(BF16)


def data_terms(value):
    top, rest = split(value)
    return jnp.concatenate([top, rest, top], axis=0)


def one_hot(index, rows, value):
    place = lax.broadcasted_iota(jnp.int16, (rows, index.shape[1]), 0)
    return jnp.where(place == index.astype(jnp.int16), value, jnp.zeros((), BF16))


def deposit_kernel(cell_ref, charge_ref, out_ref):
    cell = cell_ref[...]
    row = ((cell >> 6) & 31) * 8 + (cell >> 13)
    column = ((cell >> 11) & 3) * 64 + (cell & 63)
    out_ref[...] = lax.dot_general(
        one_hot(row, 256, jnp.ones((), BF16)),
        one_hot(column, 256, charge_ref[...]),
        (((1,), (1,)), ((), ())),
        preferred_element_type=F32,
    )


def deposit(cells, charge):
    return pl.pallas_call(
        deposit_kernel,
        out_shape=jax.ShapeDtypeStruct((256, 256), F32),
        compiler_params=pltpu.CompilerParams(vmem_limit_bytes=48 * 2**20),
        name="deposit",
    )(cells, charge)


def spectral_kernel(
    order_ref,
    density_ref,
    green_ref,
    z_ref,
    x_ref,
    y_ref,
    iz_hi_ref,
    iz_lo_ref,
    iy_ref,
    ix_ref,
    out_ref,
    after_z,
    after_x,
    total,
    back,
):
    step = pl.program_id(0)
    top, rest = split(density_ref[0])
    for low in range(4):
        lanes = slice(low * GZ, (low + 1) * GZ)
        terms = jnp.concatenate([top[:, lanes], rest[:, lanes], top[:, lanes]], axis=1)
        after_z[:, 2 * MZ * low : 2 * MZ * (low + 1)] = dot(terms, z_ref[...])
    for pair in range(GY // 2):
        sides = []
        for y in (2 * pair, 2 * pair + 1):
            tiles = [
                after_z[8 * y : 8 * y + 8, (2 * low + part) * MZ : (2 * low + part + 1) * MZ]
                for part in range(2)
                for low in range(4)
            ]
            sides.append(jnp.concatenate(tiles, axis=0))
        out = dot(x_ref[...], data_terms(jnp.concatenate(sides, axis=1)))
        for side in range(2):
            rows = pl.ds((2 * pair + side) * PITCH_X, 2 * MX)
            after_x[rows, :] = out[:, side * MZ : (side + 1) * MZ]

    @pl.when(step == 0)
    def _():
        total[...] = jnp.zeros_like(total)

    width = green_ref.shape[3]
    for pair in range(MX // 2):
        sides = []
        for kx in (2 * pair, 2 * pair + 1):
            real = after_x[pl.ds(kx, GY, stride=PITCH_X), :]
            imag = after_x[pl.ds(MX + kx, GY, stride=PITCH_X), :]
            sides.append(jnp.concatenate([real, imag], axis=0))
        out = dot(y_ref[0], data_terms(jnp.concatenate(sides, axis=1)))
        for side in range(2):
            kx = 2 * pair + side
            real = out[:width, side * MZ : (side + 1) * MZ]
            imag = out[width:, side * MZ : (side + 1) * MZ]
            green_real = green_ref[0, 0, kx]
            green_imag = green_ref[0, 1, kx]
            rows = pl.ds(kx * width, width)
            total[rows, :MZ] += green_real * real - green_imag * imag
            total[rows, MZ:] += green_real * imag + green_imag * real

    @pl.when(step == pl.num_programs(0) - 1)
    def _():
        lane = lax.broadcasted_iota(jnp.int32, (GY, 2 * GZ), 1)
        first = lane < GZ
        for group in range(MX // 8):
            top, rest = split(total[group * 8 * width : (group + 1) * 8 * width, :])
            turned = dot(top, iz_hi_ref[...]) + (
                dot(rest, iz_hi_ref[...]) + dot(top, iz_lo_ref[...])
            )
            for pair in range(4):
                sides = [
                    turned[(2 * pair + side) * width : (2 * pair + side + 1) * width, :]
                    for side in range(2)
                ]
                out = dot(iy_ref[0], data_terms(jnp.concatenate(sides, axis=1)))
                for side in range(2):
                    kx = group * 8 + 2 * pair + side
                    by_cos = out[:GY, side * MZ : (side + 1) * MZ]
                    by_sin = pltpu.roll(out[GY:, side * MZ : (side + 1) * MZ], GZ, 1)
                    back[pl.ds(kx * PITCH_Y, GY), :] = by_cos + jnp.where(
                        first, -by_sin, by_sin
                    )
        for pair in range(GY // 2):
            sides = [back[pl.ds(2 * pair + side, MX, stride=PITCH_Y), :] for side in range(2)]
            out = dot(ix_ref[...], data_terms(jnp.concatenate(sides, axis=1)))
            even = out[:GX, :MZ] - pltpu.roll(out[GX:, :MZ], GZ, 1)
            odd = pltpu.roll(out[:GX, MZ:], GZ, 1) - out[GX:, MZ:]
            out_ref[pair * GX : (pair + 1) * GX, :] = jnp.where(first, even, odd)


def spectral(order, densities, green, tables):
    offsets, _, _, width, _ = green.shape

    def whole(table):
        return pl.BlockSpec(table.shape, lambda i, order: (0,) * table.ndim)

    def by_pencil(table):
        return pl.BlockSpec((1,) + table.shape[1:], lambda i, order: (order[offsets], 0, 0))

    return pl.pallas_call(
        spectral_kernel,
        grid_spec=pltpu.PrefetchScalarGridSpec(
            num_scalar_prefetch=1,
            grid=(offsets,),
            in_specs=[
                pl.BlockSpec((1, 256, 256), lambda i, order: (i, 0, 0)),
                pl.BlockSpec((1, 2, MX, width, MZ), lambda i, order: (order[i], 0, 0, 0, 0)),
                whole(tables["z"]),
                whole(tables["x"]),
                by_pencil(tables["y"]),
                whole(tables["iz_hi"]),
                whole(tables["iz_lo"]),
                by_pencil(tables["iy"]),
                whole(tables["ix"]),
            ],
            out_specs=pl.BlockSpec((512, 128), lambda i, order: (0, 0)),
            scratch_shapes=[
                pltpu.VMEM((256, 1024), F32),
                pltpu.VMEM((GY * PITCH_X, MZ), F32),
                pltpu.VMEM((MX * width, 2 * MZ), F32),
                pltpu.VMEM((MX * PITCH_Y, 2 * GZ), F32),
            ],
        ),
        out_shape=jax.ShapeDtypeStruct((512, 128), F32),
        compiler_params=pltpu.CompilerParams(vmem_limit_bytes=48 * 2**20),
        name="spectral",
    )(
        order,
        densities,
        green,
        *(tables[name] for name in ("z", "x", "y", "iz_hi", "iz_lo", "iy", "ix")),
    )


def gather_kernel(own_ref, other_ref, cell_ref, out_ref, field):
    potential = own_ref[...] + other_ref[...]
    lane = lax.broadcasted_iota(jnp.int32, (512, 128), 1)
    row = lax.broadcasted_iota(jnp.int32, (512, 128), 0)
    x = row % GX
    z = lane % GZ
    zero = jnp.zeros((GX, 128), F32)
    below = jnp.where(x == 0, 0.0, pltpu.roll(potential, 1, 0))
    above = jnp.where(x == GX - 1, 0.0, pltpu.roll(potential, 511, 0))
    field_x = 0.5 * (below - above)
    turned = pltpu.roll(potential, GZ, 1)
    before = jnp.concatenate([zero, turned[: 512 - GX]], axis=0)
    after = jnp.concatenate([turned[GX:], zero], axis=0)
    field_y = 0.5 * (
        jnp.where(lane < GZ, before, turned) - jnp.where(lane < GZ, turned, after)
    )
    left = jnp.where(z == 0, 0.0, pltpu.roll(potential, 1, 1))
    right = jnp.where(z == GZ - 1, 0.0, pltpu.roll(potential, 127, 1))
    field_z = 0.5 * (left - right)
    for part, value in enumerate((field_x, field_y, field_z)):
        field[part * 128 : (part + 1) * 128, :] = jnp.transpose(value).astype(BF16)

    count = cell_ref.shape[1]
    chunk = min(GATHER_CHUNK, count)
    for at in range(0, count, chunk):
        cell = cell_ref[:, at : at + chunk]
        y = (cell >> 6) & 31
        high = (y >> 1) * GX + (cell >> 11)
        low = (y & 1) * GZ + (cell & 63)
        picked = dot(field[...], one_hot(high, 512, jnp.ones((), BF16)))
        inside = lax.broadcasted_iota(jnp.int32, (128, chunk), 0) == low
        for part in range(3):
            values = jnp.where(inside, picked[part * 128 : (part + 1) * 128], 0.0)
            out_ref[part, :, at : at + chunk] = jnp.sum(values, axis=0, keepdims=True)


def gather(own, other, cells):
    return pl.pallas_call(
        gather_kernel,
        out_shape=jax.ShapeDtypeStruct((3, 1, cells.shape[1]), F32),
        scratch_shapes=[pltpu.VMEM((384, 512), BF16)],
        compiler_params=pltpu.CompilerParams(vmem_limit_bytes=48 * 2**20),
        name="gather",
    )(own, other, cells)


def per_device(tables, charge, cell_deposit, cell_gather, green_spectra):
    pencils = lax.axis_size("pencil")
    bunches = lax.axis_size("bunch")
    pencil = lax.axis_index("pencil")
    swap = [(i, (i + 1) % pencils) for i in range(pencils)]
    part = deposit(cell_deposit, charge)
    density = part + lax.ppermute(part, "pencil", swap)
    near = []
    for distance in range(SPAN, 0, -1):
        route = []
        for bunch in range(distance, bunches):
            ends = (bunch * pencils, (bunch - distance) * pencils + 1)
            route.extend([ends, ends[::-1]])
        near.append(lax.ppermute(density, ("bunch", "pencil"), route))
    near = jnp.stack(near)
    far = lax.ppermute(near, "pencil", swap)
    densities = jnp.concatenate([density[None], near, far], axis=0)
    steps = np.arange(SPAN, 0, -1)
    up = np.concatenate([[SPAN], SPAN + steps, SPAN - steps, [0]])
    down = np.concatenate([[SPAN], SPAN - steps, SPAN + steps, [1]])
    order = jnp.where(pencil == 0, jnp.asarray(up, jnp.int32), jnp.asarray(down, jnp.int32))
    own = spectral(order, densities, green_spectra, tables)
    other = lax.ppermute(own, "pencil", swap)
    return gather(own, other, cell_gather)


def solution(mesh):
    in_specs = (
        P(("groups", "bunch"), "pencil"),
        P(("groups", "bunch"), "pencil"),
        P(("groups", "bunch"), "pencil"),
        P(None, None, None, "pencil", None),
    )
    out_specs = P(None, ("groups", "bunch"), "pencil")
    tables = make_tables(mesh.shape["pencil"])
    return jax.shard_map(
        functools.partial(per_device, tables),
        mesh=mesh,
        in_specs=in_specs,
        out_specs=out_specs,
        check_vma=False,
    )
```

```python
import functools

import jax
import jax.numpy as jnp
import numpy as np
from jax import lax
from jax.experimental import pallas as pl
from jax.experimental.pallas import tpu as pltpu
from jax.sharding import PartitionSpec as P

GX = 32
GY = 32
GZ = 64
SPAN = 3
MX = 64
MY = 64
MZ = 128
BF16 = jnp.bfloat16
F32 = jnp.float32
CHARGE_BITS = 12
CHARGE_UNITS = 512.0
GATHER_CHUNK = 512
PITCH_X = 2 * MX + 1
PITCH_Y = GY + 1
KX_BLOCK = 16
VMEM_LIMIT = 36 * 2**20
STAGE_FLOPS = 2 * 3 * (1024 * 64 * 256 + 2 * 2048 * 64 * 64)


def hi_lo(table):
    top = table.astype(np.float32).astype(BF16)
    rest = (table - top.astype(np.float64)).astype(np.float32).astype(BF16)
    return top, rest


def stacked_terms(table):
    top, rest = hi_lo(table)
    return np.concatenate([top, top, rest], axis=-1)


def phases(rows, columns, period):
    angles = 2.0 * np.pi / period * ((rows[:, None] * columns[None, :]) % period)
    return np.cos(angles), np.sin(angles)


def make_tables(pencils):
    width = MY // pencils
    cos_z, sin_z = phases(np.arange(GZ), np.arange(MZ), MZ)
    forward_z = np.concatenate([cos_z, -sin_z], axis=1)
    grid_x = (np.arange(8)[None, :] * 4 + np.arange(4)[:, None]).reshape(-1)
    cos_x, sin_x = phases(np.arange(MX), grid_x, MX)
    forward_x = np.block([[cos_x, sin_x], [-sin_x, cos_x]])
    forward_y = []
    inverse_y = []
    for pencil in range(pencils):
        own = np.arange(pencil * width, (pencil + 1) * width)
        cos_y, sin_y = phases(own, np.arange(GY), MY)
        forward_y.append(stacked_terms(np.block([[cos_y, sin_y], [-sin_y, cos_y]])))
        inverse_y.append(stacked_terms(np.concatenate([cos_y.T, sin_y.T], axis=0)))
    cos_b, sin_b = phases(np.arange(MZ), np.arange(GZ), MZ)
    inverse_z = np.block([[cos_b, sin_b], [-sin_b, cos_b]])
    cos_c, sin_c = phases(np.arange(GX), np.arange(MX), MX)
    inverse_x = np.concatenate([cos_c, sin_c], axis=0) / float(MX * MY * MZ)
    tables = dict(
        z=stacked_terms(forward_z.T).T,
        x=stacked_terms(forward_x),
        y=np.concatenate(forward_y),
        iz=np.concatenate(hi_lo(inverse_z), axis=1),
        iy=np.concatenate(inverse_y),
        ix=stacked_terms(inverse_x),
    )
    places = {}
    packed = []
    at = 0
    for name, table in tables.items():
        rows, columns = table.shape
        places[name] = (at, rows // (pencils if name in ("y", "iy") else 1), columns)
        packed.append(np.pad(table, ((0, 0), (0, 256 - columns))))
        at += rows
    return np.concatenate(packed), places


def in_hbm(array):
    return pltpu.with_memory_space_constraint(array, pltpu.HBM)


def in_vmem(array):
    return pltpu.with_memory_space_constraint(array, pltpu.VMEM)


def dot(a, b):
    return jnp.dot(a, b, preferred_element_type=F32)


def split(value):
    top = value.astype(BF16)
    return top, (value - top.astype(F32)).astype(BF16)


def data_terms(value):
    top, rest = split(value)
    return jnp.concatenate([top, rest, top], axis=0)


def one_hot(index, rows, value):
    place = lax.broadcasted_iota(jnp.int16, (rows, index.shape[1]), 0)
    return jnp.where(place == index.astype(jnp.int16), value, jnp.zeros((), BF16))


def deposit_kernel(particles_ref, table_hbm, out_ref, table_ref, arrived):
    copy = pltpu.make_async_copy(table_hbm, table_ref, arrived)
    copy.start()
    particles = particles_ref[...]
    cell = particles >> CHARGE_BITS
    charge = (particles & (2**CHARGE_BITS - 1)).astype(F32) * (1.0 / CHARGE_UNITS)
    row = ((cell >> 6) & 31) * 8 + (cell >> 13)
    column = ((cell >> 11) & 3) * 64 + (cell & 63)
    out_ref[...] = lax.dot_general(
        one_hot(row, 256, jnp.ones((), BF16)),
        one_hot(column, 256, charge.astype(BF16)),
        (((1,), (1,)), ((), ())),
        preferred_element_type=F32,
    )
    copy.wait()


def deposit(cells, charge, packed):
    units = (charge.astype(F32) * CHARGE_UNITS).astype(jnp.int32)
    particles = (cells << CHARGE_BITS) + units
    return pl.pallas_call(
        deposit_kernel,
        in_specs=[
            pl.BlockSpec(memory_space=pltpu.VMEM),
            pl.BlockSpec(memory_space=pltpu.HBM),
        ],
        out_specs=[pl.BlockSpec(memory_space=pltpu.VMEM)] * 2,
        out_shape=[
            jax.ShapeDtypeStruct((256, 256), F32),
            jax.ShapeDtypeStruct(packed.shape, packed.dtype),
        ],
        scratch_shapes=[pltpu.SemaphoreType.DMA],
        compiler_params=pltpu.CompilerParams(vmem_limit_bytes=VMEM_LIMIT),
        name="deposit",
    )(in_vmem(particles), in_hbm(jnp.asarray(packed)))


def table_rows(table_ref, places, name, pencil=None):
    start, rows, columns = places[name]
    if pencil is not None:
        start = pl.multiple_of(start + pencil * rows, 16)
    return table_ref[pl.ds(start, rows), :columns]


def stage_zx(density, table_z, table_x, after_z, after_x, at):
    top, rest = split(density)
    for low in range(4):
        lanes = slice(low * GZ, (low + 1) * GZ)
        terms = jnp.concatenate([top[:, lanes], rest[:, lanes], top[:, lanes]], axis=1)
        after_z[:, 2 * MZ * low : 2 * MZ * (low + 1)] = dot(terms, table_z)
    for pair in range(GY // 2):
        sides = []
        for y in (2 * pair, 2 * pair + 1):
            tiles = [
                after_z[8 * y : 8 * y + 8, (2 * low + part) * MZ : (2 * low + part + 1) * MZ]
                for part in range(2)
                for low in range(4)
            ]
            sides.append(jnp.concatenate(tiles, axis=0))
        out = dot(table_x, data_terms(jnp.concatenate(sides, axis=1)))
        for side in range(2):
            rows = pl.ds((2 * pair + side) * PITCH_X, 2 * MX)
            after_x[at, rows, :] = out[:, side * MZ : (side + 1) * MZ]


def spectral_kernel(places, offsets, first, last, *refs):
    refs = list(refs)
    count = len(offsets)
    densities = [refs.pop(0) for _ in range(count)]
    green_ref = refs.pop(0)
    table_ref = refs.pop(0)
    before_ref = None if first else refs.pop(0)
    out_ref = refs.pop(0)
    after_z = refs.pop(0)
    after_x = refs.pop(0)
    green = refs.pop(0)
    arrived = refs.pop(0)
    total, back = (refs.pop(0), refs.pop(0)) if last else (out_ref, None)
    width = green_ref.shape[3]
    block = KX_BLOCK
    pencil = lax.axis_index("pencil")
    sign = 1 - 2 * pencil

    def copy(at, step):
        kx = pl.ds(step * block, block)
        return pltpu.make_async_copy(
            green_ref.at[SPAN + sign * offsets[at], :, kx], green.at[at, :, kx], arrived.at[at, step]
        )

    for step in range(MX // block):
        for at in range(count):
            copy(at, step).start()

    def table(name):
        return table_rows(table_ref, places, name, pencil if name in ("y", "iy") else None)

    for at, density_ref in enumerate(densities):
        stage_zx(density_ref[...], table("z"), table("x"), after_z, after_x, at)

    def kx_block(step):
        for at in range(count):
            copy(at, step).wait()
        for pair in range(block // 2):
            sums = [[None, None], [None, None]]
            starts = [
                pl.multiple_of((step * block + 2 * pair + side) * width, width) for side in range(2)
            ]
            if not first:
                for side in range(2):
                    rows = pl.ds(starts[side], width)
                    sums[side] = [before_ref[rows, :MZ], before_ref[rows, MZ:]]
            for at in range(count):
                sides = []
                for side in range(2):
                    kx = step * block + 2 * pair + side
                    real = after_x[at, pl.ds(kx, GY, stride=PITCH_X), :]
                    imag = after_x[at, pl.ds(MX + kx, GY, stride=PITCH_X), :]
                    sides.append(jnp.concatenate([real, imag], axis=0))
                out = dot(table("y"), data_terms(jnp.concatenate(sides, axis=1)))
                for side in range(2):
                    kx = step * block + 2 * pair + side
                    real = out[:width, side * MZ : (side + 1) * MZ]
                    imag = out[width:, side * MZ : (side + 1) * MZ]
                    green_real = green[at, 0, kx]
                    green_imag = green[at, 1, kx]
                    terms = (
                        green_real * real - green_imag * imag,
                        green_real * imag + green_imag * real,
                    )
                    for part in range(2):
                        held = sums[side][part]
                        sums[side][part] = terms[part] if held is None else held + terms[part]
            for side in range(2):
                rows = pl.ds(starts[side], width)
                total[rows, :MZ] = sums[side][0]
                total[rows, MZ:] = sums[side][1]

    pl.loop(0, MX // block)(kx_block)
    if not last:
        return

    lane = lax.broadcasted_iota(jnp.int32, (GY, 2 * GZ), 1)
    front = lane < GZ

    lane = lax.broadcasted_iota(jnp.int32, (GY, 2 * GZ), 1)
    front = lane < GZ
    def back_block(step):
        start = pl.multiple_of(step * block * width, block * width)
        top, rest = split(total[pl.ds(start, block * width), :])
        both = table("iz")
        wide = dot(top, both)
        turned = wide[:, : 2 * GZ] + (wide[:, 2 * GZ :] + dot(rest, both[:, : 2 * GZ]))
        for pair in range(block // 2):
            sides = [
                turned[(2 * pair + side) * width : (2 * pair + side + 1) * width, :]
                for side in range(2)
            ]
            out = dot(table("iy"), data_terms(jnp.concatenate(sides, axis=1)))
            for side in range(2):
                kx = step * block + 2 * pair + side
                by_cos = out[:GY, side * 2 * GZ : (side + 1) * 2 * GZ]
                by_sin = pltpu.roll(out[GY:, side * 2 * GZ : (side + 1) * 2 * GZ], GZ, 1)
                back[pl.ds(kx * PITCH_Y, GY), :] = by_cos + jnp.where(front, -by_sin, by_sin)

    pl.loop(0, MX // block)(back_block)
    for pair in range(GY // 2):
        sides = [back[pl.ds(2 * pair + side, MX, stride=PITCH_Y), :] for side in range(2)]
        out = dot(table("ix"), data_terms(jnp.concatenate(sides, axis=1)))
        even = out[:GX, : 2 * GZ] - pltpu.roll(out[GX:, : 2 * GZ], GZ, 1)
        odd = pltpu.roll(out[:GX, 2 * GZ :], GZ, 1) - out[GX:, 2 * GZ :]
        out_ref[pair * GX : (pair + 1) * GX, :] = jnp.where(front, even, odd)


def spectral(offsets, densities, green, tables, before, last):
    count = len(densities)
    first = before is None
    width = green.shape[3]
    packed, places = tables
    scratch = [
        pltpu.VMEM((256, 1024), F32),
        pltpu.VMEM((count, GY * PITCH_X, MZ), F32),
        pltpu.VMEM((count,) + green.shape[1:], F32),
        pltpu.SemaphoreType.DMA((count, MX // KX_BLOCK)),
    ]
    out_shape = jax.ShapeDtypeStruct((MX * width, 2 * MZ), F32)
    if last:
        scratch.append(pltpu.VMEM((MX * width, 2 * MZ), F32))
        scratch.append(pltpu.VMEM((MX * PITCH_Y, 2 * GZ), F32))
        out_shape = jax.ShapeDtypeStruct((512, 128), F32)
    vmem = pl.BlockSpec(memory_space=pltpu.VMEM)
    return pl.pallas_call(
        functools.partial(spectral_kernel, places, offsets, first, last),
        in_specs=[
            *([vmem] * count),
            pl.BlockSpec(memory_space=pltpu.HBM),
            vmem,
            *([] if first else [vmem]),
        ],
        out_specs=vmem,
        scratch_shapes=scratch,
        out_shape=out_shape,
        compiler_params=pltpu.CompilerParams(vmem_limit_bytes=VMEM_LIMIT),
        cost_estimate=pl.CostEstimate(
            flops=2 * count * STAGE_FLOPS, bytes_accessed=count * 2**21, transcendentals=0
        ),
        name="spectral_last" if last else "spectral_part",
    )(
        *map(in_vmem, densities),
        in_hbm(green),
        in_vmem(packed),
        *([] if first else [in_vmem(before)]),
    )


def gather_kernel(own_ref, other_ref, cell_ref, out_ref, field):
    potential = own_ref[...] + other_ref[...]
    lane = lax.broadcasted_iota(jnp.int32, (512, 128), 1)
    row = lax.broadcasted_iota(jnp.int32, (512, 128), 0)
    x = row % GX
    z = lane % GZ
    zero = jnp.zeros((GX, 128), F32)
    below = jnp.where(x == 0, 0.0, pltpu.roll(potential, 1, 0))
    above = jnp.where(x == GX - 1, 0.0, pltpu.roll(potential, 511, 0))
    field_x = 0.5 * (below - above)
    turned = pltpu.roll(potential, GZ, 1)
    before = jnp.concatenate([zero, turned[: 512 - GX]], axis=0)
    after = jnp.concatenate([turned[GX:], zero], axis=0)
    field_y = 0.5 * (
        jnp.where(lane < GZ, before, turned) - jnp.where(lane < GZ, turned, after)
    )
    left = jnp.where(z == 0, 0.0, pltpu.roll(potential, 1, 1))
    right = jnp.where(z == GZ - 1, 0.0, pltpu.roll(potential, 127, 1))
    field_z = 0.5 * (left - right)
    for part, value in enumerate((field_x, field_y, field_z)):
        field[part * 128 : (part + 1) * 128, :] = jnp.transpose(value).astype(BF16)

    count = cell_ref.shape[1]
    chunk = min(GATHER_CHUNK, count)
    for at in range(0, count, chunk):
        cell = cell_ref[:, at : at + chunk]
        y = (cell >> 6) & 31
        high = (y >> 1) * GX + (cell >> 11)
        low = (y & 1) * GZ + (cell & 63)
        picked = dot(field[...], one_hot(high, 512, jnp.ones((), BF16)))
        inside = lax.broadcasted_iota(jnp.int32, (128, chunk), 0) == low
        for part in range(3):
            values = jnp.where(inside, picked[part * 128 : (part + 1) * 128], 0.0)
            out_ref[part, :, at : at + chunk] = jnp.sum(values, axis=0, keepdims=True)


def gather(own, other, cells):
    return pl.pallas_call(
        gather_kernel,
        out_shape=jax.ShapeDtypeStruct((3, 1, cells.shape[1]), F32),
        scratch_shapes=[pltpu.VMEM((384, 512), BF16)],
        compiler_params=pltpu.CompilerParams(vmem_limit_bytes=48 * 2**20),
        name="gather",
    )(own, other, cells)


def per_device(tables, charge, cell_deposit, cell_gather, green_spectra):
    pencils = lax.axis_size("pencil")
    bunches = lax.axis_size("bunch")
    swap = [(i, (i + 1) % pencils) for i in range(pencils)]
    packed, places = tables
    part, packed = deposit(cell_deposit, charge, packed)
    tables = (packed, places)
    density = part + lax.ppermute(part, "pencil", swap)
    near = []
    for distance in range(SPAN, 0, -1):
        route = []
        for bunch in range(distance, bunches):
            ends = (bunch * pencils, (bunch - distance) * pencils + 1)
            route.extend([ends, ends[::-1]])
        near.append(lax.ppermute(density, ("bunch", "pencil"), route))
    steps = tuple(range(SPAN, 0, -1))
    back_steps = tuple(-step for step in steps)

    def terms(offsets, densities, before, last):
        return spectral(offsets, densities, green_spectra, tables, before, last)

    total = terms((0,), [density], None, False)
    total, near[0] = lax.optimization_barrier((total, near[0]))
    far = [lax.ppermute(each, "pencil", swap) for each in near[:-1]]
    total = terms(steps[:-1], near[:-1], total, False)
    total, near[-1] = lax.optimization_barrier((total, near[-1]))
    far.append(lax.ppermute(near[-1], "pencil", swap))
    total = terms(steps[-1:], near[-1:], total, False)
    own = terms(back_steps, far, total, True)
    other = lax.ppermute(own, "pencil", swap)
    return gather(own, other, cell_gather)


def solution(mesh):
    in_specs = (
        P(("groups", "bunch"), "pencil"),
        P(("groups", "bunch"), "pencil"),
        P(("groups", "bunch"), "pencil"),
        P(None, None, None, "pencil", None),
    )
    out_specs = P(None, ("groups", "bunch"), "pencil")
    tables = make_tables(mesh.shape["pencil"])
    return jax.shard_map(
        functools.partial(per_device, tables),
        mesh=mesh,
        in_specs=in_specs,
        out_specs=out_specs,
        check_vma=False,
    )
```

```python
import functools
import math

import jax
import jax.numpy as jnp
import numpy as np
from jax import lax
from jax.experimental import pallas as pl
from jax.experimental.pallas import tpu as pltpu
from jax.sharding import PartitionSpec as P

GX = 32
GY = 32
GZ = 64
SPAN = 3
MX = 64
MY = 64
MZ = 128
BF16 = jnp.bfloat16
F32 = jnp.float32
MOST_CHARGE = 4.0
CHARGE_BITS = 12
CHARGE_UNITS = 512.0
GATHER_CHUNK = 512
PITCH_X = 2 * MX + 1
PITCH_Y = GY + 1
KX_BLOCK = 16
NEAR_GROUPS = ((0,), (1, 2))
VMEM_LIMIT = 36 * 2**20
STAGE_FLOPS = 2 * 3 * (1024 * 64 * 256 + 2 * 2048 * 64 * 64)


def hi_lo(table):
    top = table.astype(np.float32).astype(BF16)
    rest = (table - top.astype(np.float64)).astype(np.float32).astype(BF16)
    return top, rest


def stacked_terms(table):
    top, rest = hi_lo(table)
    return np.concatenate([top, top, rest], axis=-1)


def phases(rows, columns, period):
    angles = 2.0 * np.pi / period * ((rows[:, None] * columns[None, :]) % period)
    return np.cos(angles), np.sin(angles)


def make_tables(pencils):
    width = MY // pencils
    cos_z, sin_z = phases(np.arange(GZ), np.arange(MZ), MZ)
    forward_z = np.concatenate([cos_z, -sin_z], axis=1)
    grid_x = (np.arange(8)[None, :] * 4 + np.arange(4)[:, None]).reshape(-1)
    cos_x, sin_x = phases(np.arange(MX), grid_x, MX)
    forward_x = np.block([[cos_x, sin_x], [-sin_x, cos_x]])
    forward_y = []
    inverse_y = []
    for pencil in range(pencils):
        own = np.arange(pencil * width, (pencil + 1) * width)
        cos_y, sin_y = phases(own, np.arange(GY), MY)
        forward_y.append(stacked_terms(np.block([[cos_y, sin_y], [-sin_y, cos_y]])))
        inverse_y.append(stacked_terms(np.concatenate([cos_y.T, sin_y.T], axis=0)))
    cos_b, sin_b = phases(np.arange(MZ), np.arange(GZ), MZ)
    inverse_z = np.block([[cos_b, sin_b], [-sin_b, cos_b]])
    cos_c, sin_c = phases(np.arange(GX), np.arange(MX), MX)
    inverse_x = np.concatenate([cos_c, sin_c], axis=0) / float(MX * MY * MZ)
    tables = dict(
        z=stacked_terms(forward_z.T).T,
        x=stacked_terms(forward_x),
        y=np.concatenate(forward_y),
        iz=np.concatenate(hi_lo(inverse_z), axis=1),
        iy=np.concatenate(inverse_y),
        ix=stacked_terms(inverse_x),
    )
    places = {}
    packed = []
    at = 0
    for name, table in tables.items():
        rows, columns = table.shape
        places[name] = (at, rows // (pencils if name in ("y", "iy") else 1), columns)
        packed.append(np.pad(table, ((0, 0), (0, 256 - columns))))
        at += rows
    return np.concatenate(packed), places


def exchange_rounds(bunches, pencils):
    if bunches == 8 and pencils == 2 and SPAN == 3:
        cycles = (((0, 1, 3, 5, 7, 6, 4, 2),), ((0, 3, 2), (7, 4, 5)), ((1, 2, 5, 6, 3, 4),))
        rounds = []
        for round_cycles in cycles:
            seen = [0] * bunches
            pairs = []
            for cycle in round_cycles:
                for start, end in zip(cycle, cycle[1:] + cycle[:1]):
                    pairs.append((start * 2 + seen[start], end * 2 + seen[end]))
                    seen[start] += 1
                    seen[end] += 1
            pairs += [(2 * bunch, 2 * bunch + 1) for bunch in range(bunches) if not seen[bunch]]
            rounds.append(pairs)
        return rounds
    return [
        [(bunch * pencils, (bunch - distance) * pencils + 1) for bunch in range(distance, bunches)]
        for distance in range(SPAN, 0, -1)
    ]


def round_offsets(rounds, bunches, pencils):
    met = [{bunch} for bunch in range(bunches)]
    tables = []
    for pairs in rounds:
        offsets = [0] * (bunches * pencils)
        counts = [0] * (bunches * pencils)
        for pair in pairs:
            for here, there in (pair, pair[::-1]):
                bunch, source = here // pencils, there // pencils
                if abs(bunch - source) <= SPAN and source not in met[bunch]:
                    met[bunch].add(source)
                    offsets[here] = bunch - source
                    counts[here] = 1
        tables.append((offsets, counts))
    for bunch in range(bunches):
        assert met[bunch] == {b for b in range(bunches) if abs(b - bunch) <= SPAN}
    return tables


def lookup(values, index):
    found = jnp.int32(values[0])
    for at, value in enumerate(values):
        if value != values[0]:
            found = jnp.where(index == at, jnp.int32(value), found)
    return found


def in_hbm(array):
    return pltpu.with_memory_space_constraint(array, pltpu.HBM)


def in_vmem(array):
    return pltpu.with_memory_space_constraint(array, pltpu.VMEM)


def dot(a, b):
    return jnp.dot(a, b, preferred_element_type=F32)


def split(value):
    top = value.astype(BF16)
    return top, (value - top.astype(F32)).astype(BF16)


def data_terms(value):
    top, rest = split(value)
    return jnp.concatenate([top, rest, top], axis=0)


def one_hot(index, rows, value):
    place = lax.broadcasted_iota(jnp.int16, (rows, index.shape[1]), 0)
    return jnp.where(place == index.astype(jnp.int16), value, jnp.zeros((), BF16))


def deposit_kernel(particles_ref, table_hbm, out_ref, table_ref, arrived):
    copy = pltpu.make_async_copy(table_hbm, table_ref, arrived)
    copy.start()
    particles = particles_ref[...]
    cell = particles >> CHARGE_BITS
    charge = (particles & (2**CHARGE_BITS - 1)).astype(F32) * (1.0 / CHARGE_UNITS)
    row = ((cell >> 6) & 31) * 8 + (cell >> 13)
    column = ((cell >> 11) & 3) * 64 + (cell & 63)
    out_ref[...] = lax.dot_general(
        one_hot(row, 256, jnp.ones((), BF16)),
        one_hot(column, 256, charge.astype(BF16)),
        (((1,), (1,)), ((), ())),
        preferred_element_type=F32,
    )
    copy.wait()


def deposit(cells, charge, packed):
    units = (charge.astype(F32) * CHARGE_UNITS).astype(jnp.int32)
    particles = (cells << CHARGE_BITS) + units
    return pl.pallas_call(
        deposit_kernel,
        in_specs=[
            pl.BlockSpec(memory_space=pltpu.VMEM),
            pl.BlockSpec(memory_space=pltpu.HBM),
        ],
        out_specs=[pl.BlockSpec(memory_space=pltpu.VMEM)] * 2,
        out_shape=[
            jax.ShapeDtypeStruct((256, 256), F32),
            jax.ShapeDtypeStruct(packed.shape, packed.dtype),
        ],
        scratch_shapes=[pltpu.SemaphoreType.DMA],
        compiler_params=pltpu.CompilerParams(vmem_limit_bytes=VMEM_LIMIT),
        name="deposit",
    )(in_vmem(particles), in_hbm(jnp.asarray(packed)))


def table_rows(table_ref, places, name, pencil=None):
    start, rows, columns = places[name]
    if pencil is not None:
        start = pl.multiple_of(start + pencil * rows, 16)
    return table_ref[pl.ds(start, rows), :columns]


def stage_zx(density, table_z, table_x, after_z, after_x, at):
    top, rest = split(density)
    for low in range(4):
        lanes = slice(low * GZ, (low + 1) * GZ)
        terms = jnp.concatenate([top[:, lanes], rest[:, lanes], top[:, lanes]], axis=1)
        after_z[:, 2 * MZ * low : 2 * MZ * (low + 1)] = dot(terms, table_z)
    for pair in range(GY // 2):
        sides = []
        for y in (2 * pair, 2 * pair + 1):
            tiles = [
                after_z[8 * y : 8 * y + 8, (2 * low + part) * MZ : (2 * low + part + 1) * MZ]
                for part in range(2)
                for low in range(4)
            ]
            sides.append(jnp.concatenate(tiles, axis=0))
        out = dot(table_x, data_terms(jnp.concatenate(sides, axis=1)))
        for side in range(2):
            rows = pl.ds((2 * pair + side) * PITCH_X, 2 * MX)
            after_x[at, rows, :] = out[:, side * MZ : (side + 1) * MZ]


def spectral_kernel(places, offsets, first, last, *refs):
    refs = list(refs)
    count = len(offsets)
    densities = [refs.pop(0) for _ in range(count)]
    green_ref = refs.pop(0)
    table_ref = refs.pop(0)
    before_ref = None if first else refs.pop(0)
    out_ref = refs.pop(0)
    after_z = refs.pop(0)
    after_x = refs.pop(0)
    green = refs.pop(0)
    arrived = refs.pop(0)
    total, back = (refs.pop(0), refs.pop(0)) if last else (out_ref, None)
    width = green_ref.shape[3]
    block = KX_BLOCK
    pencil = lax.axis_index("pencil")
    device = lax.axis_index("bunch") * lax.axis_size("pencil") + pencil
    chosen = [SPAN + lookup(values, device) for values, _ in offsets]

    def copy(at, step):
        kx = pl.ds(step * block, block)
        return pltpu.make_async_copy(
            green_ref.at[chosen[at], :, kx], green.at[at, :, kx], arrived.at[at, step]
        )

    for step in range(MX // block):
        for at in range(count):
            copy(at, step).start()

    def table(name):
        return table_rows(table_ref, places, name, pencil if name in ("y", "iy") else None)

    for at, density_ref in enumerate(densities):
        density = density_ref[...]
        if min(offsets[at][1]) == 0:
            density = density * lookup(offsets[at][1], device).astype(F32)
        stage_zx(density, table("z"), table("x"), after_z, after_x, at)

    def kx_block(step):
        for at in range(count):
            copy(at, step).wait()
        for pair in range(block // 2):
            sums = [[None, None], [None, None]]
            starts = [
                pl.multiple_of((step * block + 2 * pair + side) * width, width) for side in range(2)
            ]
            if not first:
                for side in range(2):
                    rows = pl.ds(starts[side], width)
                    sums[side] = [before_ref[rows, :MZ], before_ref[rows, MZ:]]
            for at in range(count):
                sides = []
                for side in range(2):
                    kx = step * block + 2 * pair + side
                    real = after_x[at, pl.ds(kx, GY, stride=PITCH_X), :]
                    imag = after_x[at, pl.ds(MX + kx, GY, stride=PITCH_X), :]
                    sides.append(jnp.concatenate([real, imag], axis=0))
                out = dot(table("y"), data_terms(jnp.concatenate(sides, axis=1)))
                for side in range(2):
                    kx = step * block + 2 * pair + side
                    real = out[:width, side * MZ : (side + 1) * MZ]
                    imag = out[width:, side * MZ : (side + 1) * MZ]
                    green_real = green[at, 0, kx]
                    green_imag = green[at, 1, kx]
                    terms = (
                        green_real * real - green_imag * imag,
                        green_real * imag + green_imag * real,
                    )
                    for part in range(2):
                        held = sums[side][part]
                        sums[side][part] = terms[part] if held is None else held + terms[part]
            for side in range(2):
                rows = pl.ds(starts[side], width)
                total[rows, :MZ] = sums[side][0]
                total[rows, MZ:] = sums[side][1]

    pl.loop(0, MX // block)(kx_block)
    if not last:
        return

    lane = lax.broadcasted_iota(jnp.int32, (GY, 2 * GZ), 1)
    front = lane < GZ

    lane = lax.broadcasted_iota(jnp.int32, (GY, 2 * GZ), 1)
    front = lane < GZ
    def back_block(step):
        start = pl.multiple_of(step * block * width, block * width)
        top, rest = split(total[pl.ds(start, block * width), :])
        both = table("iz")
        wide = dot(top, both)
        turned = wide[:, : 2 * GZ] + (wide[:, 2 * GZ :] + dot(rest, both[:, : 2 * GZ]))
        for pair in range(block // 2):
            sides = [
                turned[(2 * pair + side) * width : (2 * pair + side + 1) * width, :]
                for side in range(2)
            ]
            out = dot(table("iy"), data_terms(jnp.concatenate(sides, axis=1)))
            for side in range(2):
                kx = step * block + 2 * pair + side
                by_cos = out[:GY, side * 2 * GZ : (side + 1) * 2 * GZ]
                by_sin = pltpu.roll(out[GY:, side * 2 * GZ : (side + 1) * 2 * GZ], GZ, 1)
                back[pl.ds(kx * PITCH_Y, GY), :] = by_cos + jnp.where(front, -by_sin, by_sin)

    pl.loop(0, MX // block)(back_block)
    for pair in range(GY // 2):
        sides = [back[pl.ds(2 * pair + side, MX, stride=PITCH_Y), :] for side in range(2)]
        out = dot(table("ix"), data_terms(jnp.concatenate(sides, axis=1)))
        even = out[:GX, : 2 * GZ] - pltpu.roll(out[GX:, : 2 * GZ], GZ, 1)
        odd = pltpu.roll(out[:GX, 2 * GZ :], GZ, 1) - out[GX:, 2 * GZ :]
        out_ref[pair * GX : (pair + 1) * GX, :] = jnp.where(front, even, odd)


def spectral(offsets, densities, green, tables, before, last):
    count = len(densities)
    first = before is None
    width = green.shape[3]
    packed, places = tables
    scratch = [
        pltpu.VMEM((256, 1024), F32),
        pltpu.VMEM((count, GY * PITCH_X, MZ), F32),
        pltpu.VMEM((count,) + green.shape[1:], F32),
        pltpu.SemaphoreType.DMA((count, MX // KX_BLOCK)),
    ]
    out_shape = jax.ShapeDtypeStruct((MX * width, 2 * MZ), F32)
    if last:
        scratch.append(pltpu.VMEM((MX * width, 2 * MZ), F32))
        scratch.append(pltpu.VMEM((MX * PITCH_Y, 2 * GZ), F32))
        out_shape = jax.ShapeDtypeStruct((512, 128), F32)
    vmem = pl.BlockSpec(memory_space=pltpu.VMEM)
    return pl.pallas_call(
        functools.partial(spectral_kernel, places, offsets, first, last),
        in_specs=[
            *([vmem] * count),
            pl.BlockSpec(memory_space=pltpu.HBM),
            vmem,
            *([] if first else [vmem]),
        ],
        out_specs=vmem,
        scratch_shapes=scratch,
        out_shape=out_shape,
        compiler_params=pltpu.CompilerParams(vmem_limit_bytes=VMEM_LIMIT),
        cost_estimate=pl.CostEstimate(
            flops=2 * count * STAGE_FLOPS, bytes_accessed=count * 2**21, transcendentals=0
        ),
        name="spectral_last" if last else "spectral_part",
    )(
        *map(in_vmem, densities),
        in_hbm(green),
        in_vmem(packed),
        *([] if first else [in_vmem(before)]),
    )


def gather_kernel(own_ref, other_ref, cell_ref, out_ref, field):
    potential = own_ref[...] + other_ref[...]
    lane = lax.broadcasted_iota(jnp.int32, (512, 128), 1)
    row = lax.broadcasted_iota(jnp.int32, (512, 128), 0)
    x = row % GX
    z = lane % GZ
    zero = jnp.zeros((GX, 128), F32)
    below = jnp.where(x == 0, 0.0, pltpu.roll(potential, 1, 0))
    above = jnp.where(x == GX - 1, 0.0, pltpu.roll(potential, 511, 0))
    field_x = 0.5 * (below - above)
    turned = pltpu.roll(potential, GZ, 1)
    before = jnp.concatenate([zero, turned[: 512 - GX]], axis=0)
    after = jnp.concatenate([turned[GX:], zero], axis=0)
    field_y = 0.5 * (
        jnp.where(lane < GZ, before, turned) - jnp.where(lane < GZ, turned, after)
    )
    left = jnp.where(z == 0, 0.0, pltpu.roll(potential, 1, 1))
    right = jnp.where(z == GZ - 1, 0.0, pltpu.roll(potential, 127, 1))
    field_z = 0.5 * (left - right)
    for part, value in enumerate((field_x, field_y, field_z)):
        field[part * 128 : (part + 1) * 128, :] = jnp.transpose(value).astype(BF16)

    count = cell_ref.shape[1]
    chunk = min(GATHER_CHUNK, count)
    for at in range(0, count, chunk):
        cell = cell_ref[:, at : at + chunk]
        y = (cell >> 6) & 31
        high = (y >> 1) * GX + (cell >> 11)
        low = (y & 1) * GZ + (cell & 63)
        picked = dot(field[...], one_hot(high, 512, jnp.ones((), BF16)))
        inside = lax.broadcasted_iota(jnp.int32, (128, chunk), 0) == low
        for part in range(3):
            values = jnp.where(inside, picked[part * 128 : (part + 1) * 128], 0.0)
            out_ref[part, :, at : at + chunk] = jnp.sum(values, axis=0, keepdims=True)


def gather(own, other, cells):
    return pl.pallas_call(
        gather_kernel,
        out_shape=jax.ShapeDtypeStruct((3, 1, cells.shape[1]), F32),
        scratch_shapes=[pltpu.VMEM((384, 512), BF16)],
        compiler_params=pltpu.CompilerParams(vmem_limit_bytes=48 * 2**20),
        name="gather",
    )(own, other, cells)


def per_device(tables, charge, cell_deposit, cell_gather, green_spectra):
    pencils = lax.axis_size("pencil")
    bunches = lax.axis_size("bunch")
    swap = [(i, (i + 1) % pencils) for i in range(pencils)]
    packed, places = tables
    part, packed = deposit(cell_deposit, charge, packed)
    tables = (packed, places)
    density = part + lax.ppermute(part, "pencil", swap)
    rounds = exchange_rounds(bunches, pencils)
    offsets = round_offsets(rounds, bunches, pencils)
    particles = charge.shape[1] * pencils
    scale = 2.0 ** (15 - math.ceil(math.log2(particles * MOST_CHARGE)))
    sent = (density * scale).astype(jnp.float16)
    near = []
    for pairs in rounds:
        route = [*pairs, *(pair[::-1] for pair in pairs)]
        near.append(lax.ppermute(sent, ("bunch", "pencil"), route))

    def received(array):
        return array.astype(F32) * (1.0 / scale)

    def terms(offsets, densities, before, last):
        return spectral(offsets, densities, green_spectra, tables, before, last)

    devices = bunches * pencils
    total = terms([([0] * devices, [1] * devices)], [density], None, False)
    far = []
    for group in NEAR_GROUPS:
        arrivals = [near[at] for at in group]
        total, arrivals = lax.optimization_barrier((total, arrivals))
        far += [lax.ppermute(each, "pencil", swap) for each in arrivals]
        arrivals = [received(each) for each in arrivals]
        total = terms([offsets[at] for at in group], arrivals, total, False)

    def beside(values):
        return [values[bunch * pencils + (core + 1) % pencils] for bunch in range(bunches) for core in range(pencils)]

    far_offsets = [tuple(map(beside, offsets[at])) for group in NEAR_GROUPS for at in group]
    own = terms(far_offsets, [received(each) for each in far], total, True)
    other = lax.ppermute(own, "pencil", swap)
    return gather(own, other, cell_gather)


def solution(mesh):
    in_specs = (
        P(("groups", "bunch"), "pencil"),
        P(("groups", "bunch"), "pencil"),
        P(("groups", "bunch"), "pencil"),
        P(None, None, None, "pencil", None),
    )
    out_specs = P(None, ("groups", "bunch"), "pencil")
    tables = make_tables(mesh.shape["pencil"])
    return jax.shard_map(
        functools.partial(per_device, tables),
        mesh=mesh,
        in_specs=in_specs,
        out_specs=out_specs,
        check_vma=False,
    )
```

```python
import functools
import math

import jax
import jax.numpy as jnp
import numpy as np
from jax import lax
from jax.experimental import pallas as pl
from jax.experimental.pallas import tpu as pltpu
from jax.sharding import PartitionSpec as P

GX = 32
GY = 32
GZ = 64
SPAN = 3
MX = 64
MY = 64
MZ = 128
BF16 = jnp.bfloat16
F32 = jnp.float32
MOST_CHARGE = 4.0
CHARGE_BITS = 12
CHARGE_UNITS = 512.0
GATHER_CHUNK = 512
PITCH_X = 2 * MX + 1
PITCH_Y = GY + 1
KX_BLOCK = 32
NEAR_GROUPS = ((0,), (1, 2))
VMEM_LIMIT = 36 * 2**20
STAGE_FLOPS = 2 * 3 * (1024 * 64 * 256 + 2 * 2048 * 64 * 64)


def hi_lo(table):
    top = table.astype(np.float32).astype(BF16)
    rest = (table - top.astype(np.float64)).astype(np.float32).astype(BF16)
    return top, rest


def stacked_terms(table):
    top, rest = hi_lo(table)
    return np.concatenate([top, top, rest], axis=-1)


def stacked_rows(table):
    top, rest = hi_lo(table)
    return np.block([[top, top], [rest, np.zeros_like(rest)]])


def phases(rows, columns, period):
    angles = 2.0 * np.pi / period * ((rows[:, None] * columns[None, :]) % period)
    return np.cos(angles), np.sin(angles)


def make_tables(pencils):
    width = MY // pencils
    cos_z, sin_z = phases(np.arange(GZ), np.arange(MZ), MZ)
    forward_z = np.concatenate([cos_z, -sin_z], axis=1)
    grid_x = (np.arange(8)[None, :] * 4 + np.arange(4)[:, None]).reshape(-1)
    cos_x, sin_x = phases(np.arange(MX), grid_x, MX)
    forward_x = np.block([[cos_x, sin_x], [-sin_x, cos_x]])
    forward_y = []
    inverse_y = []
    for pencil in range(pencils):
        own = np.arange(pencil * width, (pencil + 1) * width)
        cos_y, sin_y = phases(own, np.arange(GY), MY)
        forward_y.append(stacked_rows(np.block([[cos_y, sin_y], [-sin_y, cos_y]])))
        inverse_y.append(stacked_terms(np.concatenate([cos_y.T, sin_y.T], axis=0)))
    cos_b, sin_b = phases(np.arange(MZ), np.arange(GZ), MZ)
    inverse_z = np.block([[cos_b, sin_b], [-sin_b, cos_b]])
    cos_c, sin_c = phases(np.arange(GX), np.arange(MX), MX)
    inverse_x = np.concatenate([cos_c, sin_c], axis=0) / float(MX * MY * MZ)
    tables = dict(
        z=stacked_terms(forward_z.T).T,
        x=stacked_terms(forward_x),
        y=np.concatenate(forward_y),
        iz=np.concatenate(hi_lo(inverse_z), axis=1),
        iy=np.concatenate(inverse_y),
        ix=stacked_terms(inverse_x),
    )
    places = {}
    packed = []
    at = 0
    for name, table in tables.items():
        rows, columns = table.shape
        places[name] = (at, rows // (pencils if name in ("y", "iy") else 1), columns)
        packed.append(np.pad(table, ((0, 0), (0, 256 - columns))))
        at += rows
    return np.concatenate(packed), places


def exchange_rounds(bunches, pencils):
    if bunches == 8 and pencils == 2 and SPAN == 3:
        cycles = (((0, 1, 3, 5, 7, 6, 4, 2),), ((0, 3, 2), (7, 4, 5)), ((1, 2, 5, 6, 3, 4),))
        rounds = []
        for round_cycles in cycles:
            seen = [0] * bunches
            pairs = []
            for cycle in round_cycles:
                for start, end in zip(cycle, cycle[1:] + cycle[:1]):
                    pairs.append((start * 2 + seen[start], end * 2 + seen[end]))
                    seen[start] += 1
                    seen[end] += 1
            pairs += [(2 * bunch, 2 * bunch + 1) for bunch in range(bunches) if not seen[bunch]]
            rounds.append(pairs)
        return rounds
    return [
        [(bunch * pencils, (bunch - distance) * pencils + 1) for bunch in range(distance, bunches)]
        for distance in range(SPAN, 0, -1)
    ]


def round_offsets(rounds, bunches, pencils):
    met = [{bunch} for bunch in range(bunches)]
    tables = []
    for pairs in rounds:
        offsets = [0] * (bunches * pencils)
        counts = [0] * (bunches * pencils)
        for pair in pairs:
            for here, there in (pair, pair[::-1]):
                bunch, source = here // pencils, there // pencils
                if abs(bunch - source) <= SPAN and source not in met[bunch]:
                    met[bunch].add(source)
                    offsets[here] = bunch - source
                    counts[here] = 1
        tables.append((offsets, counts))
    for bunch in range(bunches):
        assert met[bunch] == {b for b in range(bunches) if abs(b - bunch) <= SPAN}
    return tables


def lookup(values, index):
    found = jnp.int32(values[0])
    for at, value in enumerate(values):
        if value != values[0]:
            found = jnp.where(index == at, jnp.int32(value), found)
    return found


def in_hbm(array):
    return pltpu.with_memory_space_constraint(array, pltpu.HBM)


def in_vmem(array):
    return pltpu.with_memory_space_constraint(array, pltpu.VMEM)


def dot(a, b):
    return jnp.dot(a, b, preferred_element_type=F32)


def split(value):
    top = value.astype(BF16)
    return top, (value - top.astype(F32)).astype(BF16)


def data_terms(value):
    top, rest = split(value)
    return jnp.concatenate([top, rest, top], axis=0)


def one_hot(index, rows, value):
    place = lax.broadcasted_iota(jnp.int16, (rows, index.shape[1]), 0)
    return jnp.where(place == index.astype(jnp.int16), value, jnp.zeros((), BF16))


def two_term_dot(table, value):
    out = dot(table, jnp.concatenate(split(value), axis=0))
    half = out.shape[0] // 2
    return out[:half] + out[half:]


def deposit_kernel(particles_ref, table_hbm, out_ref, table_ref, arrived):
    copy = pltpu.make_async_copy(table_hbm, table_ref, arrived)
    copy.start()
    particles = particles_ref[...]
    cell = particles >> CHARGE_BITS
    charge = (particles & (2**CHARGE_BITS - 1)).astype(F32) * (1.0 / CHARGE_UNITS)
    row = ((cell >> 6) & 31) * 8 + (cell >> 13)
    column = ((cell >> 11) & 3) * 64 + (cell & 63)
    out_ref[...] = lax.dot_general(
        one_hot(row, 256, jnp.ones((), BF16)),
        one_hot(column, 256, charge.astype(BF16)),
        (((1,), (1,)), ((), ())),
        preferred_element_type=F32,
    )
    copy.wait()


def deposit(cells, charge, packed):
    units = (charge.astype(F32) * CHARGE_UNITS).astype(jnp.int32)
    particles = (cells << CHARGE_BITS) + units
    return pl.pallas_call(
        deposit_kernel,
        in_specs=[
            pl.BlockSpec(memory_space=pltpu.VMEM),
            pl.BlockSpec(memory_space=pltpu.HBM),
        ],
        out_specs=[pl.BlockSpec(memory_space=pltpu.VMEM)] * 2,
        out_shape=[
            jax.ShapeDtypeStruct((256, 256), F32),
            jax.ShapeDtypeStruct(packed.shape, packed.dtype),
        ],
        scratch_shapes=[pltpu.SemaphoreType.DMA],
        compiler_params=pltpu.CompilerParams(vmem_limit_bytes=VMEM_LIMIT),
        name="deposit",
    )(in_vmem(particles), in_hbm(jnp.asarray(packed)))


def table_rows(table_ref, places, name, pencil=None):
    start, rows, columns = places[name]
    if pencil is not None:
        start = pl.multiple_of(start + pencil * rows, 16)
    return table_ref[pl.ds(start, rows), :columns]


def stage_zx(density, table_z, table_x, after_z, after_x, at):
    top, rest = split(density)
    for low in range(4):
        lanes = slice(low * GZ, (low + 1) * GZ)
        terms = jnp.concatenate([top[:, lanes], rest[:, lanes], top[:, lanes]], axis=1)
        after_z[:, 2 * MZ * low : 2 * MZ * (low + 1)] = dot(terms, table_z)
    for pair in range(GY // 2):
        sides = []
        for y in (2 * pair, 2 * pair + 1):
            tiles = [
                after_z[8 * y : 8 * y + 8, (2 * low + part) * MZ : (2 * low + part + 1) * MZ]
                for part in range(2)
                for low in range(4)
            ]
            sides.append(jnp.concatenate(tiles, axis=0))
        out = dot(table_x, data_terms(jnp.concatenate(sides, axis=1)))
        for side in range(2):
            rows = pl.ds((2 * pair + side) * PITCH_X, 2 * MX)
            after_x[at, rows, :] = out[:, side * MZ : (side + 1) * MZ]


def spectral_kernel(places, offsets, first, last, *refs):
    refs = list(refs)
    count = len(offsets)
    densities = [refs.pop(0) for _ in range(count)]
    green_ref = refs.pop(0)
    table_ref = refs.pop(0)
    before_ref = None if first else refs.pop(0)
    out_ref = refs.pop(0)
    after_z = refs.pop(0)
    after_x = refs.pop(0)
    green = refs.pop(0)
    arrived = refs.pop(0)
    total, back = (refs.pop(0), refs.pop(0)) if last else (out_ref, None)
    width = green_ref.shape[3]
    block = KX_BLOCK
    pencil = lax.axis_index("pencil")
    device = lax.axis_index("bunch") * lax.axis_size("pencil") + pencil
    chosen = [SPAN + lookup(values, device) for values, _ in offsets]

    def copy(at, step):
        kx = pl.ds(step * block, block)
        return pltpu.make_async_copy(
            green_ref.at[chosen[at], :, kx], green.at[at, :, kx], arrived.at[at, step]
        )

    for step in range(MX // block):
        for at in range(count):
            copy(at, step).start()

    def table(name):
        return table_rows(table_ref, places, name, pencil if name in ("y", "iy") else None)

    for at, density_ref in enumerate(densities):
        density = density_ref[...]
        if min(offsets[at][1]) == 0:
            density = density * lookup(offsets[at][1], device).astype(F32)
        stage_zx(density, table("z"), table("x"), after_z, after_x, at)

    def kx_block(step):
        for at in range(count):
            copy(at, step).wait()
        for pair in range(block // 2):
            sums = [[None, None], [None, None]]
            starts = [
                pl.multiple_of((step * block + 2 * pair + side) * width, width) for side in range(2)
            ]
            if not first:
                for side in range(2):
                    rows = pl.ds(starts[side], width)
                    sums[side] = [before_ref[rows, :MZ], before_ref[rows, MZ:]]
            for at in range(count):
                sides = []
                for side in range(2):
                    kx = step * block + 2 * pair + side
                    real = after_x[at, pl.ds(kx, GY, stride=PITCH_X), :]
                    imag = after_x[at, pl.ds(MX + kx, GY, stride=PITCH_X), :]
                    sides.append(jnp.concatenate([real, imag], axis=0))
                out = two_term_dot(table("y"), jnp.concatenate(sides, axis=1))
                for side in range(2):
                    kx = step * block + 2 * pair + side
                    real = out[:width, side * MZ : (side + 1) * MZ]
                    imag = out[width:, side * MZ : (side + 1) * MZ]
                    green_real = green[at, 0, kx]
                    green_imag = green[at, 1, kx]
                    terms = (
                        green_real * real - green_imag * imag,
                        green_real * imag + green_imag * real,
                    )
                    for part in range(2):
                        held = sums[side][part]
                        sums[side][part] = terms[part] if held is None else held + terms[part]
            for side in range(2):
                rows = pl.ds(starts[side], width)
                total[rows, :MZ] = sums[side][0]
                total[rows, MZ:] = sums[side][1]

    pl.loop(0, MX // block)(kx_block)
    if not last:
        return

    lane = lax.broadcasted_iota(jnp.int32, (GY, 2 * GZ), 1)
    front = lane < GZ

    lane = lax.broadcasted_iota(jnp.int32, (GY, 2 * GZ), 1)
    front = lane < GZ
    def back_block(step):
        start = pl.multiple_of(step * block * width, block * width)
        top, rest = split(total[pl.ds(start, block * width), :])
        both = table("iz")
        wide = dot(top, both)
        turned = wide[:, : 2 * GZ] + (wide[:, 2 * GZ :] + dot(rest, both[:, : 2 * GZ]))
        for pair in range(block // 2):
            sides = [
                turned[(2 * pair + side) * width : (2 * pair + side + 1) * width, :]
                for side in range(2)
            ]
            out = dot(table("iy"), data_terms(jnp.concatenate(sides, axis=1)))
            for side in range(2):
                kx = step * block + 2 * pair + side
                by_cos = out[:GY, side * 2 * GZ : (side + 1) * 2 * GZ]
                by_sin = pltpu.roll(out[GY:, side * 2 * GZ : (side + 1) * 2 * GZ], GZ, 1)
                back[pl.ds(kx * PITCH_Y, GY), :] = by_cos + jnp.where(front, -by_sin, by_sin)

    pl.loop(0, MX // block)(back_block)
    for pair in range(GY // 2):
        sides = [back[pl.ds(2 * pair + side, MX, stride=PITCH_Y), :] for side in range(2)]
        out = dot(table("ix"), data_terms(jnp.concatenate(sides, axis=1)))
        even = out[:GX, : 2 * GZ] - pltpu.roll(out[GX:, : 2 * GZ], GZ, 1)
        odd = pltpu.roll(out[:GX, 2 * GZ :], GZ, 1) - out[GX:, 2 * GZ :]
        out_ref[pair * GX : (pair + 1) * GX, :] = jnp.where(front, even, odd)


def spectral(offsets, densities, green, tables, before, last):
    count = len(densities)
    first = before is None
    width = green.shape[3]
    packed, places = tables
    scratch = [
        pltpu.VMEM((256, 1024), F32),
        pltpu.VMEM((count, GY * PITCH_X, MZ), F32),
        pltpu.VMEM((count,) + green.shape[1:], F32),
        pltpu.SemaphoreType.DMA((count, MX // KX_BLOCK)),
    ]
    out_shape = jax.ShapeDtypeStruct((MX * width, 2 * MZ), F32)
    if last:
        scratch.append(pltpu.VMEM((MX * width, 2 * MZ), F32))
        scratch.append(pltpu.VMEM((MX * PITCH_Y, 2 * GZ), F32))
        out_shape = jax.ShapeDtypeStruct((512, 128), F32)
    vmem = pl.BlockSpec(memory_space=pltpu.VMEM)
    return pl.pallas_call(
        functools.partial(spectral_kernel, places, offsets, first, last),
        in_specs=[
            *([vmem] * count),
            pl.BlockSpec(memory_space=pltpu.HBM),
            vmem,
            *([] if first else [vmem]),
        ],
        out_specs=vmem,
        scratch_shapes=scratch,
        out_shape=out_shape,
        compiler_params=pltpu.CompilerParams(vmem_limit_bytes=VMEM_LIMIT),
        cost_estimate=pl.CostEstimate(
            flops=2 * count * STAGE_FLOPS, bytes_accessed=count * 2**21, transcendentals=0
        ),
        name="spectral_last" if last else "spectral_part",
    )(
        *map(in_vmem, densities),
        in_hbm(green),
        in_vmem(packed),
        *([] if first else [in_vmem(before)]),
    )


def gather_kernel(own_ref, other_ref, cell_ref, out_ref, field):
    potential = own_ref[...] + other_ref[...]
    lane = lax.broadcasted_iota(jnp.int32, (512, 128), 1)
    row = lax.broadcasted_iota(jnp.int32, (512, 128), 0)
    x = row % GX
    z = lane % GZ
    zero = jnp.zeros((GX, 128), F32)
    below = jnp.where(x == 0, 0.0, pltpu.roll(potential, 1, 0))
    above = jnp.where(x == GX - 1, 0.0, pltpu.roll(potential, 511, 0))
    field_x = 0.5 * (below - above)
    turned = pltpu.roll(potential, GZ, 1)
    before = jnp.concatenate([zero, turned[: 512 - GX]], axis=0)
    after = jnp.concatenate([turned[GX:], zero], axis=0)
    field_y = 0.5 * (
        jnp.where(lane < GZ, before, turned) - jnp.where(lane < GZ, turned, after)
    )
    left = jnp.where(z == 0, 0.0, pltpu.roll(potential, 1, 1))
    right = jnp.where(z == GZ - 1, 0.0, pltpu.roll(potential, 127, 1))
    field_z = 0.5 * (left - right)
    for part, value in enumerate((field_x, field_y, field_z)):
        field[part * 128 : (part + 1) * 128, :] = jnp.transpose(value).astype(BF16)

    count = cell_ref.shape[1]
    chunk = min(GATHER_CHUNK, count)
    for at in range(0, count, chunk):
        cell = cell_ref[:, at : at + chunk]
        y = (cell >> 6) & 31
        high = (y >> 1) * GX + (cell >> 11)
        low = (y & 1) * GZ + (cell & 63)
        picked = dot(field[...], one_hot(high, 512, jnp.ones((), BF16)))
        inside = lax.broadcasted_iota(jnp.int32, (128, chunk), 0) == low
        for part in range(3):
            values = jnp.where(inside, picked[part * 128 : (part + 1) * 128], 0.0)
            out_ref[part, :, at : at + chunk] = jnp.sum(values, axis=0, keepdims=True)


def gather(own, other, cells):
    return pl.pallas_call(
        gather_kernel,
        out_shape=jax.ShapeDtypeStruct((3, 1, cells.shape[1]), F32),
        scratch_shapes=[pltpu.VMEM((384, 512), BF16)],
        compiler_params=pltpu.CompilerParams(vmem_limit_bytes=48 * 2**20),
        name="gather",
    )(own, other, cells)


def per_device(tables, charge, cell_deposit, cell_gather, green_spectra):
    pencils = lax.axis_size("pencil")
    bunches = lax.axis_size("bunch")
    swap = [(i, (i + 1) % pencils) for i in range(pencils)]
    packed, places = tables
    part, packed = deposit(cell_deposit, charge, packed)
    tables = (packed, places)
    density = part + lax.ppermute(part, "pencil", swap)
    rounds = exchange_rounds(bunches, pencils)
    offsets = round_offsets(rounds, bunches, pencils)
    particles = charge.shape[1] * pencils
    scale = 2.0 ** (15 - math.ceil(math.log2(particles * MOST_CHARGE)))
    sent = (density * scale).astype(jnp.float16)
    near = []
    for pairs in rounds:
        route = [*pairs, *(pair[::-1] for pair in pairs)]
        near.append(lax.ppermute(sent, ("bunch", "pencil"), route))

    def received(array):
        return array.astype(F32) * (1.0 / scale)

    def terms(offsets, densities, before, last):
        return spectral(offsets, densities, green_spectra, tables, before, last)

    devices = bunches * pencils
    total = terms([([0] * devices, [1] * devices)], [density], None, False)
    far = []
    for group in NEAR_GROUPS:
        arrivals = [near[at] for at in group]
        total, arrivals = lax.optimization_barrier((total, arrivals))
        far += [lax.ppermute(each, "pencil", swap) for each in arrivals]
        arrivals = [received(each) for each in arrivals]
        total = terms([offsets[at] for at in group], arrivals, total, False)

    def beside(values):
        return [values[bunch * pencils + (core + 1) % pencils] for bunch in range(bunches) for core in range(pencils)]

    far_offsets = [tuple(map(beside, offsets[at])) for group in NEAR_GROUPS for at in group]
    own = terms(far_offsets, [received(each) for each in far], total, True)
    other = lax.ppermute(own, "pencil", swap)
    return gather(own, other, cell_gather)


def solution(mesh):
    in_specs = (
        P(("groups", "bunch"), "pencil"),
        P(("groups", "bunch"), "pencil"),
        P(("groups", "bunch"), "pencil"),
        P(None, None, None, "pencil", None),
    )
    out_specs = P(None, ("groups", "bunch"), "pencil")
    tables = make_tables(mesh.shape["pencil"])
    return jax.shard_map(
        functools.partial(per_device, tables),
        mesh=mesh,
        in_specs=in_specs,
        out_specs=out_specs,
        check_vma=False,
    )
```

```python
import functools
import math

import jax
import jax.numpy as jnp
import numpy as np
from jax import lax
from jax.experimental import pallas as pl
from jax.experimental.pallas import tpu as pltpu
from jax.sharding import PartitionSpec as P

GX = 32
GY = 32
GZ = 64
SPAN = 3
MX = 64
MY = 64
MZ = 128
BF16 = jnp.bfloat16
F32 = jnp.float32
MOST_CHARGE = 4.0
CHARGE_BITS = 12
CHARGE_UNITS = 512.0
GATHER_CHUNK = 512
PITCH_X = 2 * MX + 1
PITCH_Y = GY + 1
KX_BLOCK = 32
NEAR_GROUPS = ((0,), (1, 2))
VMEM_LIMIT = 36 * 2**20
STAGE_FLOPS = 2 * 3 * (1024 * 64 * 256 + 2 * 2048 * 64 * 64)


def hi_lo(table):
    top = table.astype(np.float32).astype(BF16)
    rest = (table - top.astype(np.float64)).astype(np.float32).astype(BF16)
    return top, rest


def stacked_terms(table):
    top, rest = hi_lo(table)
    return np.concatenate([top, top, rest], axis=-1)


def stacked_rows(table):
    top, rest = hi_lo(table)
    return np.block([[top, top], [rest, np.zeros_like(rest)]])


def phases(rows, columns, period):
    angles = 2.0 * np.pi / period * ((rows[:, None] * columns[None, :]) % period)
    return np.cos(angles), np.sin(angles)


def make_tables(pencils):
    width = MY // pencils
    cos_z, sin_z = phases(np.arange(GZ), np.arange(MZ), MZ)
    forward_z = np.concatenate([cos_z, -sin_z], axis=1)
    grid_x = (np.arange(8)[None, :] * 4 + np.arange(4)[:, None]).reshape(-1)
    cos_x, sin_x = phases(np.arange(MX), grid_x, MX)
    forward_x = np.block([[cos_x, sin_x], [-sin_x, cos_x]])
    forward_y = []
    inverse_y = []
    for pencil in range(pencils):
        own = np.arange(pencil * width, (pencil + 1) * width)
        cos_y, sin_y = phases(own, np.arange(GY), MY)
        forward_y.append(stacked_rows(np.block([[cos_y, sin_y], [-sin_y, cos_y]])))
        inverse_y.append(stacked_terms(np.concatenate([cos_y.T, sin_y.T], axis=0)))
    cos_b, sin_b = phases(np.arange(MZ), np.arange(GZ), MZ)
    inverse_z = np.block([[cos_b, sin_b], [-sin_b, cos_b]])
    cos_c, sin_c = phases(np.arange(GX), np.arange(MX), MX)
    inverse_x = np.concatenate([cos_c, sin_c], axis=0) / float(MX * MY * MZ)
    tables = dict(
        z=stacked_terms(forward_z.T).T,
        x=stacked_terms(forward_x),
        y=np.concatenate(forward_y),
        iz=np.concatenate(hi_lo(inverse_z), axis=1),
        iy=np.concatenate(inverse_y),
        ix=stacked_terms(inverse_x),
    )
    places = {}
    packed = []
    at = 0
    for name, table in tables.items():
        rows, columns = table.shape
        places[name] = (at, rows // (pencils if name in ("y", "iy") else 1), columns)
        packed.append(np.pad(table, ((0, 0), (0, 256 - columns))))
        at += rows
    return np.concatenate(packed), places


def exchange_rounds(bunches, pencils):
    if bunches == 8 and pencils == 2 and SPAN == 3:
        cycles = (((0, 1, 3, 5, 7, 6, 4, 2),), ((0, 3, 2), (7, 4, 5)), ((1, 2, 5, 6, 3, 4),))
        rounds = []
        for round_cycles in cycles:
            seen = [0] * bunches
            pairs = []
            for cycle in round_cycles:
                for start, end in zip(cycle, cycle[1:] + cycle[:1]):
                    pairs.append((start * 2 + seen[start], end * 2 + seen[end]))
                    seen[start] += 1
                    seen[end] += 1
            pairs += [(2 * bunch, 2 * bunch + 1) for bunch in range(bunches) if not seen[bunch]]
            rounds.append(pairs)
        return rounds
    return [
        [(bunch * pencils, (bunch - distance) * pencils + 1) for bunch in range(distance, bunches)]
        for distance in range(SPAN, 0, -1)
    ]


def round_offsets(rounds, bunches, pencils):
    met = [{bunch} for bunch in range(bunches)]
    tables = []
    for pairs in rounds:
        offsets = [0] * (bunches * pencils)
        counts = [0] * (bunches * pencils)
        for pair in pairs:
            for here, there in (pair, pair[::-1]):
                bunch, source = here // pencils, there // pencils
                if abs(bunch - source) <= SPAN and source not in met[bunch]:
                    met[bunch].add(source)
                    offsets[here] = bunch - source
                    counts[here] = 1
        tables.append((offsets, counts))
    for bunch in range(bunches):
        assert met[bunch] == {b for b in range(bunches) if abs(b - bunch) <= SPAN}
    return tables


def lookup(values, index):
    found = jnp.int32(values[0])
    for at, value in enumerate(values):
        if value != values[0]:
            found = jnp.where(index == at, jnp.int32(value), found)
    return found


def in_hbm(array):
    return pltpu.with_memory_space_constraint(array, pltpu.HBM)


def in_vmem(array):
    return pltpu.with_memory_space_constraint(array, pltpu.VMEM)


def dot(a, b):
    return jnp.dot(a, b, preferred_element_type=F32)


def split(value):
    top = value.astype(BF16)
    return top, (value - top.astype(F32)).astype(BF16)


def data_terms(value):
    top, rest = split(value)
    return jnp.concatenate([top, rest, top], axis=0)


def one_hot(index, rows, value):
    place = lax.broadcasted_iota(jnp.int16, (rows, index.shape[1]), 0)
    return jnp.where(place == index.astype(jnp.int16), value, jnp.zeros((), BF16))


def two_term_dot(table, value):
    out = dot(table, jnp.concatenate(split(value), axis=0))
    half = out.shape[0] // 2
    return out[:half] + out[half:]


def deposit_kernel(particles_ref, table_hbm, out_ref, table_ref, arrived):
    copy = pltpu.make_async_copy(table_hbm, table_ref, arrived)
    copy.start()
    particles = particles_ref[...]
    cell = particles >> CHARGE_BITS
    charge = (particles & (2**CHARGE_BITS - 1)).astype(F32) * (1.0 / CHARGE_UNITS)
    row = ((cell >> 6) & 31) * 8 + (cell >> 13)
    column = ((cell >> 11) & 3) * 64 + (cell & 63)
    out_ref[...] = lax.dot_general(
        one_hot(row, 256, jnp.ones((), BF16)),
        one_hot(column, 256, charge.astype(BF16)),
        (((1,), (1,)), ((), ())),
        preferred_element_type=F32,
    )
    copy.wait()


def deposit(cells, charge, packed):
    units = (charge.astype(F32) * CHARGE_UNITS).astype(jnp.int32)
    particles = (cells << CHARGE_BITS) + units
    return pl.pallas_call(
        deposit_kernel,
        in_specs=[
            pl.BlockSpec(memory_space=pltpu.VMEM),
            pl.BlockSpec(memory_space=pltpu.HBM),
        ],
        out_specs=[pl.BlockSpec(memory_space=pltpu.VMEM)] * 2,
        out_shape=[
            jax.ShapeDtypeStruct((256, 256), F32),
            jax.ShapeDtypeStruct(packed.shape, packed.dtype),
        ],
        scratch_shapes=[pltpu.SemaphoreType.DMA],
        compiler_params=pltpu.CompilerParams(vmem_limit_bytes=VMEM_LIMIT),
        name="deposit",
    )(in_vmem(particles), in_hbm(jnp.asarray(packed)))


def table_rows(table_ref, places, name, pencil=None):
    start, rows, columns = places[name]
    if pencil is not None:
        start = pl.multiple_of(start + pencil * rows, 16)
    return table_ref[pl.ds(start, rows), :columns]


def stage_zx(density, table_z, table_x, after_z, after_x, at):
    top, rest = split(density)
    for low in range(4):
        lanes = slice(low * GZ, (low + 1) * GZ)
        terms = jnp.concatenate([top[:, lanes], rest[:, lanes], top[:, lanes]], axis=1)
        after_z[:, 2 * MZ * low : 2 * MZ * (low + 1)] = dot(terms, table_z)
    for pair in range(GY // 2):
        sides = []
        for y in (2 * pair, 2 * pair + 1):
            tiles = [
                after_z[8 * y : 8 * y + 8, (2 * low + part) * MZ : (2 * low + part + 1) * MZ]
                for part in range(2)
                for low in range(4)
            ]
            sides.append(jnp.concatenate(tiles, axis=0))
        out = dot(table_x, data_terms(jnp.concatenate(sides, axis=1)))
        for side in range(2):
            rows = pl.ds((2 * pair + side) * PITCH_X, 2 * MX)
            after_x[at, rows, :] = out[:, side * MZ : (side + 1) * MZ]


def spectral_kernel(places, offsets, first, last, *refs):
    refs = list(refs)
    count = len(offsets)
    densities = [refs.pop(0) for _ in range(count)]
    green_ref = refs.pop(0)
    table_ref = refs.pop(0)
    before_ref = None if first else refs.pop(0)
    out_ref = refs.pop(0)
    after_z = refs.pop(0)
    after_x = refs.pop(0)
    green = refs.pop(0)
    arrived = refs.pop(0)
    total, back = (refs.pop(0), refs.pop(0)) if last else (out_ref, None)
    width = green_ref.shape[3]
    block = KX_BLOCK
    pencil = lax.axis_index("pencil")
    device = lax.axis_index("bunch") * lax.axis_size("pencil") + pencil
    chosen = [SPAN + lookup(values, device) for values, _ in offsets]

    def copy(at, step):
        kx = pl.ds(step * block, block)
        return pltpu.make_async_copy(
            green_ref.at[chosen[at], :, kx], green.at[at, :, kx], arrived.at[at, step]
        )

    for step in range(MX // block):
        for at in range(count):
            copy(at, step).start()

    def table(name):
        return table_rows(table_ref, places, name, pencil if name in ("y", "iy") else None)

    for at, density_ref in enumerate(densities):
        density = density_ref[...]
        if min(offsets[at][1]) == 0:
            density = density * lookup(offsets[at][1], device).astype(F32)
        stage_zx(density, table("z"), table("x"), after_z, after_x, at)

    def kx_block(step):
        for at in range(count):
            copy(at, step).wait()
        for pair in range(block // 2):
            sums = [[None, None], [None, None]]
            starts = [
                pl.multiple_of((step * block + 2 * pair + side) * width, width) for side in range(2)
            ]
            if not first:
                for side in range(2):
                    rows = pl.ds(starts[side], width)
                    sums[side] = [before_ref[rows, :MZ], before_ref[rows, MZ:]]
            for at in range(count):
                sides = []
                for side in range(2):
                    kx = step * block + 2 * pair + side
                    real = after_x[at, pl.ds(kx, GY, stride=PITCH_X), :]
                    imag = after_x[at, pl.ds(MX + kx, GY, stride=PITCH_X), :]
                    sides.append(jnp.concatenate([real, imag], axis=0))
                out = two_term_dot(table("y"), jnp.concatenate(sides, axis=1))
                for side in range(2):
                    kx = step * block + 2 * pair + side
                    real = out[:width, side * MZ : (side + 1) * MZ]
                    imag = out[width:, side * MZ : (side + 1) * MZ]
                    green_real = green[at, 0, kx]
                    green_imag = green[at, 1, kx]
                    terms = (
                        green_real * real - green_imag * imag,
                        green_real * imag + green_imag * real,
                    )
                    for part in range(2):
                        held = sums[side][part]
                        sums[side][part] = terms[part] if held is None else held + terms[part]
            for side in range(2):
                rows = pl.ds(starts[side], width)
                total[rows, :MZ] = sums[side][0]
                total[rows, MZ:] = sums[side][1]

    pl.loop(0, MX // block)(kx_block)
    if not last:
        return

    lane = lax.broadcasted_iota(jnp.int32, (GY, 2 * GZ), 1)
    front = lane < GZ

    lane = lax.broadcasted_iota(jnp.int32, (GY, 2 * GZ), 1)
    front = lane < GZ
    def back_block(step):
        start = pl.multiple_of(step * block * width, block * width)
        top, rest = split(total[pl.ds(start, block * width), :])
        both = table("iz")
        wide = dot(top, both)
        turned = wide[:, : 2 * GZ] + (wide[:, 2 * GZ :] + dot(rest, both[:, : 2 * GZ]))
        for pair in range(block // 2):
            sides = [
                turned[(2 * pair + side) * width : (2 * pair + side + 1) * width, :]
                for side in range(2)
            ]
            out = dot(table("iy"), data_terms(jnp.concatenate(sides, axis=1)))
            for side in range(2):
                kx = step * block + 2 * pair + side
                by_cos = out[:GY, side * 2 * GZ : (side + 1) * 2 * GZ]
                by_sin = pltpu.roll(out[GY:, side * 2 * GZ : (side + 1) * 2 * GZ], GZ, 1)
                back[pl.ds(kx * PITCH_Y, GY), :] = by_cos + jnp.where(front, -by_sin, by_sin)

    pl.loop(0, MX // block)(back_block)
    for pair in range(GY // 2):
        sides = [back[pl.ds(2 * pair + side, MX, stride=PITCH_Y), :] for side in range(2)]
        out = dot(table("ix"), data_terms(jnp.concatenate(sides, axis=1)))
        even = out[:GX, : 2 * GZ] - pltpu.roll(out[GX:, : 2 * GZ], GZ, 1)
        odd = pltpu.roll(out[:GX, 2 * GZ :], GZ, 1) - out[GX:, 2 * GZ :]
        out_ref[pair * GX : (pair + 1) * GX, :] = jnp.where(front, even, odd)


def spectral(offsets, densities, green, tables, before, last):
    count = len(densities)
    first = before is None
    width = green.shape[3]
    packed, places = tables
    scratch = [
        pltpu.VMEM((256, 1024), F32),
        pltpu.VMEM((count, GY * PITCH_X, MZ), F32),
        pltpu.VMEM((count,) + green.shape[1:], F32),
        pltpu.SemaphoreType.DMA((count, MX // KX_BLOCK)),
    ]
    out_shape = jax.ShapeDtypeStruct((MX * width, 2 * MZ), F32)
    if last:
        scratch.append(pltpu.VMEM((MX * width, 2 * MZ), F32))
        scratch.append(pltpu.VMEM((MX * PITCH_Y, 2 * GZ), F32))
        out_shape = jax.ShapeDtypeStruct((512, 128), F32)
    vmem = pl.BlockSpec(memory_space=pltpu.VMEM)
    return pl.pallas_call(
        functools.partial(spectral_kernel, places, offsets, first, last),
        in_specs=[
            *([vmem] * count),
            pl.BlockSpec(memory_space=pltpu.HBM),
            vmem,
            *([] if first else [vmem]),
        ],
        out_specs=vmem,
        scratch_shapes=scratch,
        out_shape=out_shape,
        compiler_params=pltpu.CompilerParams(vmem_limit_bytes=VMEM_LIMIT),
        cost_estimate=pl.CostEstimate(
            flops=2 * count * STAGE_FLOPS, bytes_accessed=count * 2**21, transcendentals=0
        ),
        name="spectral_last" if last else "spectral_part",
    )(
        *map(in_vmem, densities),
        in_hbm(green),
        in_vmem(packed),
        *([] if first else [in_vmem(before)]),
    )


def gather_kernel(own_ref, other_ref, cell_ref, out_ref, field):
    potential = own_ref[...] + other_ref[...]
    lane = lax.broadcasted_iota(jnp.int32, (512, 128), 1)
    row = lax.broadcasted_iota(jnp.int32, (512, 128), 0)
    x = row % GX
    z = lane % GZ
    zero = jnp.zeros((GX, 128), F32)
    below = jnp.where(x == 0, 0.0, pltpu.roll(potential, 1, 0))
    above = jnp.where(x == GX - 1, 0.0, pltpu.roll(potential, 511, 0))
    field_x = 0.5 * (below - above)
    turned = pltpu.roll(potential, GZ, 1)
    before = jnp.concatenate([zero, turned[: 512 - GX]], axis=0)
    after = jnp.concatenate([turned[GX:], zero], axis=0)
    field_y = 0.5 * (
        jnp.where(lane < GZ, before, turned) - jnp.where(lane < GZ, turned, after)
    )
    left = jnp.where(z == 0, 0.0, pltpu.roll(potential, 1, 1))
    right = jnp.where(z == GZ - 1, 0.0, pltpu.roll(potential, 127, 1))
    field_z = 0.5 * (left - right)
    for part, value in enumerate((field_x, field_y, field_z)):
        field[part * 128 : (part + 1) * 128, :] = jnp.transpose(value).astype(BF16)

    count = cell_ref.shape[1]
    chunk = min(GATHER_CHUNK, count)
    for at in range(0, count, chunk):
        cell = cell_ref[:, at : at + chunk]
        y = (cell >> 6) & 31
        high = (y >> 1) * GX + (cell >> 11)
        low = (y & 1) * GZ + (cell & 63)
        picked = dot(field[...], one_hot(high, 512, jnp.ones((), BF16)))
        inside = lax.broadcasted_iota(jnp.int32, (128, chunk), 0) == low
        for part in range(3):
            values = jnp.where(inside, picked[part * 128 : (part + 1) * 128], 0.0)
            out_ref[part, :, at : at + chunk] = jnp.sum(values, axis=0, keepdims=True)


def gather(own, other, cells):
    return pl.pallas_call(
        gather_kernel,
        out_shape=jax.ShapeDtypeStruct((3, 1, cells.shape[1]), F32),
        scratch_shapes=[pltpu.VMEM((384, 512), BF16)],
        compiler_params=pltpu.CompilerParams(vmem_limit_bytes=48 * 2**20),
        name="gather",
    )(own, other, cells)


def per_device(tables, charge, cell_deposit, cell_gather, green_spectra):
    pencils = lax.axis_size("pencil")
    bunches = lax.axis_size("bunch")
    swap = [(i, (i + 1) % pencils) for i in range(pencils)]
    packed, places = tables
    part, packed = deposit(cell_deposit, charge, packed)
    tables = (packed, places)
    particles = charge.shape[1] * pencils
    scale = 2.0 ** (15 - math.ceil(math.log2(particles * MOST_CHARGE)))
    def received(array):
        return array.astype(F32) * (1.0 / scale)

    partial = (part * scale).astype(jnp.float16)
    density = part + received(lax.ppermute(partial, "pencil", swap))
    rounds = exchange_rounds(bunches, pencils)
    offsets = round_offsets(rounds, bunches, pencils)
    sent = (density * scale).astype(jnp.float16)
    near = []
    for pairs in rounds:
        route = [*pairs, *(pair[::-1] for pair in pairs)]
        near.append(lax.ppermute(sent, ("bunch", "pencil"), route))

    def terms(offsets, densities, before, last):
        return spectral(offsets, densities, green_spectra, tables, before, last)

    devices = bunches * pencils
    total = terms([([0] * devices, [1] * devices)], [density], None, False)
    far = []
    for group in NEAR_GROUPS:
        arrivals = [near[at] for at in group]
        total, arrivals = lax.optimization_barrier((total, arrivals))
        far += [lax.ppermute(each, "pencil", swap) for each in arrivals]
        arrivals = [received(each) for each in arrivals]
        total = terms([offsets[at] for at in group], arrivals, total, False)

    def beside(values):
        return [values[bunch * pencils + (core + 1) % pencils] for bunch in range(bunches) for core in range(pencils)]

    far_offsets = [tuple(map(beside, offsets[at])) for group in NEAR_GROUPS for at in group]
    own = terms(far_offsets, [received(each) for each in far], total, True)
    other = lax.ppermute(own, "pencil", swap)
    return gather(own, other, cell_gather)


def solution(mesh):
    in_specs = (
        P(("groups", "bunch"), "pencil"),
        P(("groups", "bunch"), "pencil"),
        P(("groups", "bunch"), "pencil"),
        P(None, None, None, "pencil", None),
    )
    out_specs = P(None, ("groups", "bunch"), "pencil")
    tables = make_tables(mesh.shape["pencil"])
    return jax.shard_map(
        functools.partial(per_device, tables),
        mesh=mesh,
        in_specs=in_specs,
        out_specs=out_specs,
        check_vma=False,
    )
```

```python
import functools
import math

import jax
import jax.numpy as jnp
import numpy as np
from jax import lax
from jax.experimental import pallas as pl
from jax.experimental.pallas import tpu as pltpu
from jax.sharding import PartitionSpec as P

GX = 32
GY = 32
GZ = 64
SPAN = 3
MX = 64
MY = 64
MZ = 128
BF16 = jnp.bfloat16
F32 = jnp.float32
MOST_CHARGE = 4.0
CHARGE_BITS = 12
CHARGE_UNITS = 512.0
GATHER_CHUNK = 512
PITCH_X = 2 * MX + 1
PITCH_Y = GY + 1
KX_BLOCK = 32
NEAR_GROUPS = ((0,), (1, 2))
VMEM_LIMIT = 36 * 2**20
STAGE_FLOPS = 2 * 3 * (1024 * 64 * 256 + 2 * 2048 * 64 * 64)


def hi_lo(table):
    top = table.astype(np.float32).astype(BF16)
    rest = (table - top.astype(np.float64)).astype(np.float32).astype(BF16)
    return top, rest


def stacked_terms(table):
    top, rest = hi_lo(table)
    return np.concatenate([top, top, rest], axis=-1)


def stacked_rows(table):
    top, rest = hi_lo(table)
    return np.block([[top, top], [rest, np.zeros_like(rest)]])


def phases(rows, columns, period):
    angles = 2.0 * np.pi / period * ((rows[:, None] * columns[None, :]) % period)
    return np.cos(angles), np.sin(angles)


def make_tables(pencils):
    width = MY // pencils
    cos_z, sin_z = phases(np.arange(GZ), np.arange(MZ), MZ)
    forward_z = np.concatenate([cos_z, -sin_z], axis=1)
    grid_x = (np.arange(8)[None, :] * 4 + np.arange(4)[:, None]).reshape(-1)
    cos_x, sin_x = phases(np.arange(MX), grid_x, MX)
    forward_x = np.block([[cos_x, sin_x], [-sin_x, cos_x]])
    forward_y = []
    inverse_y = []
    for pencil in range(pencils):
        own = np.arange(pencil * width, (pencil + 1) * width)
        cos_y, sin_y = phases(own, np.arange(GY), MY)
        forward_y.append(stacked_rows(np.block([[cos_y, sin_y], [-sin_y, cos_y]])))
        inverse_y.append(stacked_terms(np.concatenate([cos_y.T, sin_y.T], axis=0)))
    cos_b, sin_b = phases(np.arange(MZ), np.arange(GZ), MZ)
    inverse_z = np.block([[cos_b, sin_b], [-sin_b, cos_b]])
    cos_c, sin_c = phases(np.arange(GX), np.arange(MX), MX)
    inverse_x = np.concatenate([cos_c, sin_c], axis=0) / float(MX * MY * MZ)
    tables = dict(
        z=stacked_terms(forward_z.T).T,
        x=stacked_terms(forward_x),
        y=np.concatenate(forward_y),
        iz=np.concatenate(hi_lo(inverse_z), axis=1),
        iy=np.concatenate(inverse_y),
        ix=stacked_terms(inverse_x),
    )
    places = {}
    packed = []
    at = 0
    for name, table in tables.items():
        rows, columns = table.shape
        places[name] = (at, rows // (pencils if name in ("y", "iy") else 1), columns)
        packed.append(np.pad(table, ((0, 0), (0, 256 - columns))))
        at += rows
    return np.concatenate(packed), places


def exchange_rounds(bunches, pencils):
    if bunches == 8 and pencils == 2 and SPAN == 3:
        cycles = (((0, 1, 3, 5, 7, 6, 4, 2),), ((0, 3, 2), (7, 4, 5)), ((1, 2, 5, 6, 3, 4),))
        rounds = []
        for round_cycles in cycles:
            seen = [0] * bunches
            pairs = []
            for cycle in round_cycles:
                for start, end in zip(cycle, cycle[1:] + cycle[:1]):
                    pairs.append((start * 2 + seen[start], end * 2 + seen[end]))
                    seen[start] += 1
                    seen[end] += 1
            pairs += [(2 * bunch, 2 * bunch + 1) for bunch in range(bunches) if not seen[bunch]]
            rounds.append(pairs)
        return rounds
    return [
        [(bunch * pencils, (bunch - distance) * pencils + 1) for bunch in range(distance, bunches)]
        for distance in range(SPAN, 0, -1)
    ]


def round_offsets(rounds, bunches, pencils):
    met = [{bunch} for bunch in range(bunches)]
    tables = []
    for pairs in rounds:
        offsets = [0] * (bunches * pencils)
        counts = [0] * (bunches * pencils)
        for pair in pairs:
            for here, there in (pair, pair[::-1]):
                bunch, source = here // pencils, there // pencils
                if abs(bunch - source) <= SPAN and source not in met[bunch]:
                    met[bunch].add(source)
                    offsets[here] = bunch - source
                    counts[here] = 1
        tables.append((offsets, counts))
    for bunch in range(bunches):
        assert met[bunch] == {b for b in range(bunches) if abs(b - bunch) <= SPAN}
    return tables


def lookup(values, index):
    found = jnp.int32(values[0])
    for at, value in enumerate(values):
        if value != values[0]:
            found = jnp.where(index == at, jnp.int32(value), found)
    return found


def in_hbm(array):
    return pltpu.with_memory_space_constraint(array, pltpu.HBM)


def in_vmem(array):
    return pltpu.with_memory_space_constraint(array, pltpu.VMEM)


def dot(a, b):
    return jnp.dot(a, b, preferred_element_type=F32)


def split(value):
    top = value.astype(BF16)
    return top, (value - top.astype(F32)).astype(BF16)


def data_terms(value):
    top, rest = split(value)
    return jnp.concatenate([top, rest, top], axis=0)


def one_hot(index, rows, value):
    place = lax.broadcasted_iota(jnp.int16, (rows, index.shape[1]), 0)
    return jnp.where(place == index.astype(jnp.int16), value, jnp.zeros((), BF16))


def two_term_dot(table, value):
    out = dot(table, jnp.concatenate(split(value), axis=0))
    half = out.shape[0] // 2
    return out[:half] + out[half:]


def deposit_kernel(particles_ref, table_hbm, out_ref, table_ref, arrived):
    copy = pltpu.make_async_copy(table_hbm, table_ref, arrived)
    copy.start()
    particles = particles_ref[...]
    cell = particles >> CHARGE_BITS
    charge = (particles & (2**CHARGE_BITS - 1)).astype(F32) * (1.0 / CHARGE_UNITS)
    row = ((cell >> 6) & 31) * 8 + (cell >> 13)
    column = ((cell >> 11) & 3) * 64 + (cell & 63)
    out_ref[...] = lax.dot_general(
        one_hot(row, 256, jnp.ones((), BF16)),
        one_hot(column, 256, charge.astype(BF16)),
        (((1,), (1,)), ((), ())),
        preferred_element_type=F32,
    )
    copy.wait()


def deposit(cells, charge, packed):
    units = (charge.astype(F32) * CHARGE_UNITS).astype(jnp.int32)
    particles = (cells << CHARGE_BITS) + units
    return pl.pallas_call(
        deposit_kernel,
        in_specs=[
            pl.BlockSpec(memory_space=pltpu.VMEM),
            pl.BlockSpec(memory_space=pltpu.HBM),
        ],
        out_specs=[pl.BlockSpec(memory_space=pltpu.VMEM)] * 2,
        out_shape=[
            jax.ShapeDtypeStruct((256, 256), F32),
            jax.ShapeDtypeStruct(packed.shape, packed.dtype),
        ],
        scratch_shapes=[pltpu.SemaphoreType.DMA],
        compiler_params=pltpu.CompilerParams(vmem_limit_bytes=VMEM_LIMIT),
        name="deposit",
    )(in_vmem(particles), in_hbm(jnp.asarray(packed)))


def table_rows(table_ref, places, name, pencil=None):
    start, rows, columns = places[name]
    if pencil is not None:
        start = pl.multiple_of(start + pencil * rows, 16)
    return table_ref[pl.ds(start, rows), :columns]


def stage_zx(density, table_z, table_x, after_z, after_x, at):
    top, rest = split(density)
    for low in range(4):
        lanes = slice(low * GZ, (low + 1) * GZ)
        terms = jnp.concatenate([top[:, lanes], rest[:, lanes], top[:, lanes]], axis=1)
        after_z[:, 2 * MZ * low : 2 * MZ * (low + 1)] = dot(terms, table_z)
    for pair in range(GY // 2):
        sides = []
        for y in (2 * pair, 2 * pair + 1):
            tiles = [
                after_z[8 * y : 8 * y + 8, (2 * low + part) * MZ : (2 * low + part + 1) * MZ]
                for part in range(2)
                for low in range(4)
            ]
            sides.append(jnp.concatenate(tiles, axis=0))
        out = dot(table_x, data_terms(jnp.concatenate(sides, axis=1)))
        for side in range(2):
            rows = pl.ds((2 * pair + side) * PITCH_X, 2 * MX)
            after_x[at, rows, :] = out[:, side * MZ : (side + 1) * MZ]


def spectral_kernel(places, offsets, first, last, *refs):
    refs = list(refs)
    count = len(offsets)
    densities = [refs.pop(0) for _ in range(count)]
    green_ref = refs.pop(0)
    table_ref = refs.pop(0)
    before_ref = None if first else refs.pop(0)
    out_ref = refs.pop(0)
    after_z = refs.pop(0)
    after_x = refs.pop(0)
    green = refs.pop(0)
    arrived = refs.pop(0)
    total, back = (refs.pop(0), refs.pop(0)) if last else (out_ref, None)
    width = green_ref.shape[3]
    block = KX_BLOCK
    pencil = lax.axis_index("pencil")
    device = lax.axis_index("bunch") * lax.axis_size("pencil") + pencil
    chosen = [SPAN + lookup(values, device) for values, _ in offsets]

    def copy(at, step):
        kx = pl.ds(step * block, block)
        return pltpu.make_async_copy(
            green_ref.at[chosen[at], :, kx], green.at[at, :, kx], arrived.at[at, step]
        )

    for step in range(MX // block):
        for at in range(count):
            copy(at, step).start()

    def table(name):
        return table_rows(table_ref, places, name, pencil if name in ("y", "iy") else None)

    for at, density_ref in enumerate(densities):
        density = density_ref[...]
        if min(offsets[at][1]) == 0:
            density = density * lookup(offsets[at][1], device).astype(F32)
        stage_zx(density, table("z"), table("x"), after_z, after_x, at)

    def kx_block(step):
        for at in range(count):
            copy(at, step).wait()
        for pair in range(block // 2):
            sums = [[None, None], [None, None]]
            starts = [
                pl.multiple_of((step * block + 2 * pair + side) * width, width) for side in range(2)
            ]
            if not first:
                for side in range(2):
                    rows = pl.ds(starts[side], width)
                    sums[side] = [before_ref[rows, :MZ], before_ref[rows, MZ:]]
            for at in range(count):
                sides = []
                for side in range(2):
                    kx = step * block + 2 * pair + side
                    real = after_x[at, pl.ds(kx, GY, stride=PITCH_X), :]
                    imag = after_x[at, pl.ds(MX + kx, GY, stride=PITCH_X), :]
                    sides.append(jnp.concatenate([real, imag], axis=0))
                out = two_term_dot(table("y"), jnp.concatenate(sides, axis=1))
                for side in range(2):
                    kx = step * block + 2 * pair + side
                    real = out[:width, side * MZ : (side + 1) * MZ]
                    imag = out[width:, side * MZ : (side + 1) * MZ]
                    green_real = green[at, 0, kx]
                    green_imag = green[at, 1, kx]
                    terms = (
                        green_real * real - green_imag * imag,
                        green_real * imag + green_imag * real,
                    )
                    for part in range(2):
                        held = sums[side][part]
                        sums[side][part] = terms[part] if held is None else held + terms[part]
            for side in range(2):
                rows = pl.ds(starts[side], width)
                total[rows, :MZ] = sums[side][0]
                total[rows, MZ:] = sums[side][1]

    pl.loop(0, MX // block)(kx_block)
    if not last:
        return

    lane = lax.broadcasted_iota(jnp.int32, (GY, 2 * GZ), 1)
    front = lane < GZ

    lane = lax.broadcasted_iota(jnp.int32, (GY, 2 * GZ), 1)
    front = lane < GZ
    def back_block(step):
        start = pl.multiple_of(step * block * width, block * width)
        top, rest = split(total[pl.ds(start, block * width), :])
        both = table("iz")
        wide = dot(top, both)
        turned = wide[:, : 2 * GZ] + (wide[:, 2 * GZ :] + dot(rest, both[:, : 2 * GZ]))
        for pair in range(block // 2):
            sides = [
                turned[(2 * pair + side) * width : (2 * pair + side + 1) * width, :]
                for side in range(2)
            ]
            out = dot(table("iy"), data_terms(jnp.concatenate(sides, axis=1)))
            for side in range(2):
                kx = step * block + 2 * pair + side
                by_cos = out[:GY, side * 2 * GZ : (side + 1) * 2 * GZ]
                by_sin = pltpu.roll(out[GY:, side * 2 * GZ : (side + 1) * 2 * GZ], GZ, 1)
                back[pl.ds(kx * PITCH_Y, GY), :] = by_cos + jnp.where(front, -by_sin, by_sin)

    pl.loop(0, MX // block)(back_block)
    for pair in range(GY // 2):
        sides = [back[pl.ds(2 * pair + side, MX, stride=PITCH_Y), :] for side in range(2)]
        out = dot(table("ix"), data_terms(jnp.concatenate(sides, axis=1)))
        even = out[:GX, : 2 * GZ] - pltpu.roll(out[GX:, : 2 * GZ], GZ, 1)
        odd = pltpu.roll(out[:GX, 2 * GZ :], GZ, 1) - out[GX:, 2 * GZ :]
        out_ref[pair * GX : (pair + 1) * GX, :] = jnp.where(front, even, odd)


def spectral(offsets, densities, green, tables, before, last):
    count = len(densities)
    first = before is None
    width = green.shape[3]
    packed, places = tables
    scratch = [
        pltpu.VMEM((256, 1024), F32),
        pltpu.VMEM((count, GY * PITCH_X, MZ), F32),
        pltpu.VMEM((count,) + green.shape[1:], F32),
        pltpu.SemaphoreType.DMA((count, MX // KX_BLOCK)),
    ]
    out_shape = jax.ShapeDtypeStruct((MX * width, 2 * MZ), F32)
    if last:
        scratch.append(pltpu.VMEM((MX * width, 2 * MZ), F32))
        scratch.append(pltpu.VMEM((MX * PITCH_Y, 2 * GZ), F32))
        out_shape = jax.ShapeDtypeStruct((512, 128), F32)
    vmem = pl.BlockSpec(memory_space=pltpu.VMEM)
    return pl.pallas_call(
        functools.partial(spectral_kernel, places, offsets, first, last),
        in_specs=[
            *([vmem] * count),
            pl.BlockSpec(memory_space=pltpu.HBM),
            vmem,
            *([] if first else [vmem]),
        ],
        out_specs=vmem,
        scratch_shapes=scratch,
        out_shape=out_shape,
        compiler_params=pltpu.CompilerParams(vmem_limit_bytes=VMEM_LIMIT),
        cost_estimate=pl.CostEstimate(
            flops=2 * count * STAGE_FLOPS, bytes_accessed=count * 2**21, transcendentals=0
        ),
        name="spectral_last" if last else "spectral_part",
    )(
        *map(in_vmem, densities),
        in_hbm(green),
        in_vmem(packed),
        *([] if first else [in_vmem(before)]),
    )


def gather_kernel(own_ref, other_ref, cell_ref, out_ref, field):
    potential = own_ref[...] + other_ref[...]
    lane = lax.broadcasted_iota(jnp.int32, (512, 128), 1)
    row = lax.broadcasted_iota(jnp.int32, (512, 128), 0)
    x = row % GX
    z = lane % GZ
    zero = jnp.zeros((GX, 128), F32)
    below = jnp.where(x == 0, 0.0, pltpu.roll(potential, 1, 0))
    above = jnp.where(x == GX - 1, 0.0, pltpu.roll(potential, 511, 0))
    field_x = 0.5 * (below - above)
    turned = pltpu.roll(potential, GZ, 1)
    before = jnp.concatenate([zero, turned[: 512 - GX]], axis=0)
    after = jnp.concatenate([turned[GX:], zero], axis=0)
    field_y = 0.5 * (
        jnp.where(lane < GZ, before, turned) - jnp.where(lane < GZ, turned, after)
    )
    left = jnp.where(z == 0, 0.0, pltpu.roll(potential, 1, 1))
    right = jnp.where(z == GZ - 1, 0.0, pltpu.roll(potential, 127, 1))
    field_z = 0.5 * (left - right)
    for part, value in enumerate((field_x, field_y, field_z)):
        field[part * 128 : (part + 1) * 128, :] = jnp.transpose(value).astype(BF16)

    count = cell_ref.shape[1]
    chunk = min(GATHER_CHUNK, count)
    for at in range(0, count, chunk):
        cell = cell_ref[:, at : at + chunk]
        y = (cell >> 6) & 31
        high = (y >> 1) * GX + (cell >> 11)
        low = (y & 1) * GZ + (cell & 63)
        picked = dot(field[...], one_hot(high, 512, jnp.ones((), BF16)))
        inside = lax.broadcasted_iota(jnp.int32, (128, chunk), 0) == low
        for part in range(3):
            values = jnp.where(inside, picked[part * 128 : (part + 1) * 128], 0.0)
            out_ref[part, :, at : at + chunk] = jnp.sum(values, axis=0, keepdims=True)


def gather(own, other, cells):
    return pl.pallas_call(
        gather_kernel,
        out_shape=jax.ShapeDtypeStruct((3, 1, cells.shape[1]), F32),
        scratch_shapes=[pltpu.VMEM((384, 512), BF16)],
        compiler_params=pltpu.CompilerParams(vmem_limit_bytes=48 * 2**20),
        name="gather",
    )(own, other, cells)


def per_device(tables, charge, cell_deposit, cell_gather, green_spectra):
    pencils = lax.axis_size("pencil")
    bunches = lax.axis_size("bunch")
    swap = [(i, (i + 1) % pencils) for i in range(pencils)]
    packed, places = tables
    part, packed = deposit(cell_deposit, charge, packed)
    tables = (packed, places)
    particles = charge.shape[1] * pencils
    scale = 2.0 ** (15 - math.ceil(math.log2(particles * MOST_CHARGE)))
    def received(array):
        return array.astype(F32) * (1.0 / scale)

    partial = (part * scale).astype(jnp.float16)
    density = part + received(lax.ppermute(partial, "pencil", swap))
    rounds = exchange_rounds(bunches, pencils)
    offsets = round_offsets(rounds, bunches, pencils)
    sent = (density * scale).astype(jnp.float16)
    near = []
    for pairs in rounds:
        route = [*pairs, *(pair[::-1] for pair in pairs)]
        near.append(lax.ppermute(sent, ("bunch", "pencil"), route))

    def terms(offsets, densities, before, last):
        return spectral(offsets, densities, green_spectra, tables, before, last)

    devices = bunches * pencils
    total = terms([([0] * devices, [1] * devices)], [density], None, False)
    far = []
    for group in NEAR_GROUPS:
        arrivals = [near[at] for at in group]
        total, arrivals = lax.optimization_barrier((total, arrivals))
        beyond = lax.ppermute(jnp.concatenate(arrivals), "pencil", swap)
        far += jnp.split(beyond, len(group))
        arrivals = [received(each) for each in arrivals]
        total = terms([offsets[at] for at in group], arrivals, total, False)

    def beside(values):
        return [values[bunch * pencils + (core + 1) % pencils] for bunch in range(bunches) for core in range(pencils)]

    far_offsets = [tuple(map(beside, offsets[at])) for group in NEAR_GROUPS for at in group]
    own = terms(far_offsets, [received(each) for each in far], total, True)
    other = lax.ppermute(own, "pencil", swap)
    return gather(own, other, cell_gather)


def solution(mesh):
    in_specs = (
        P(("groups", "bunch"), "pencil"),
        P(("groups", "bunch"), "pencil"),
        P(("groups", "bunch"), "pencil"),
        P(None, None, None, "pencil", None),
    )
    out_specs = P(None, ("groups", "bunch"), "pencil")
    tables = make_tables(mesh.shape["pencil"])
    return jax.shard_map(
        functools.partial(per_device, tables),
        mesh=mesh,
        in_specs=in_specs,
        out_specs=out_specs,
        check_vma=False,
    )
```

```python
import functools
import math

import jax
import jax.numpy as jnp
import numpy as np
from jax import lax
from jax.experimental import pallas as pl
from jax.experimental.pallas import tpu as pltpu
from jax.sharding import PartitionSpec as P

GX = 32
GY = 32
GZ = 64
SPAN = 3
MX = 64
MY = 64
MZ = 128
BF16 = jnp.bfloat16
F32 = jnp.float32
MOST_CHARGE = 4.0
CHARGE_BITS = 12
CHARGE_UNITS = 512.0
GATHER_CHUNK = 512
PITCH_X = 2 * MX + 1
PITCH_Y = GY + 1
KX_BLOCK = 32
NEAR_GROUPS = ((0,), (1, 2))
VMEM_LIMIT = 36 * 2**20
STAGE_FLOPS = 2 * 3 * (1024 * 64 * 256 + 2 * 2048 * 64 * 64)


def hi_lo(table):
    top = table.astype(np.float32).astype(BF16)
    rest = (table - top.astype(np.float64)).astype(np.float32).astype(BF16)
    return top, rest


def stacked_terms(table):
    top, rest = hi_lo(table)
    return np.concatenate([top, top, rest], axis=-1)


def stacked_rows(table):
    top, rest = hi_lo(table)
    return np.block([[top, top], [rest, np.zeros_like(rest)]])


def phases(rows, columns, period):
    angles = 2.0 * np.pi / period * ((rows[:, None] * columns[None, :]) % period)
    return np.cos(angles), np.sin(angles)


def make_tables(pencils):
    width = MY // pencils
    cos_z, sin_z = phases(np.arange(GZ), np.arange(MZ), MZ)
    forward_z = np.concatenate([cos_z, -sin_z], axis=1)
    grid_x = (np.arange(8)[None, :] * 4 + np.arange(4)[:, None]).reshape(-1)
    cos_x, sin_x = phases(np.arange(MX), grid_x, MX)
    forward_x = np.block([[cos_x, sin_x], [-sin_x, cos_x]])
    forward_y = []
    inverse_y = []
    for pencil in range(pencils):
        own = np.arange(pencil * width, (pencil + 1) * width)
        cos_y, sin_y = phases(own, np.arange(GY), MY)
        forward_y.append(stacked_rows(np.block([[cos_y, sin_y], [-sin_y, cos_y]])))
        inverse_y.append(stacked_terms(np.concatenate([cos_y.T, sin_y.T], axis=0)))
    cos_b, sin_b = phases(np.arange(MZ), np.arange(GZ), MZ)
    inverse_z = np.block([[cos_b, sin_b], [-sin_b, cos_b]])
    cos_c, sin_c = phases(np.arange(GX), np.arange(MX), MX)
    inverse_x = np.concatenate([cos_c, sin_c], axis=0) / float(MX * MY * MZ)
    tables = dict(
        z=stacked_terms(forward_z.T).T,
        x=stacked_terms(forward_x),
        y=np.concatenate(forward_y),
        iz=np.concatenate(hi_lo(inverse_z), axis=1),
        iy=np.concatenate(inverse_y),
        ix=stacked_terms(inverse_x),
    )
    places = {}
    packed = []
    at = 0
    for name, table in tables.items():
        rows, columns = table.shape
        places[name] = (at, rows // (pencils if name in ("y", "iy") else 1), columns)
        packed.append(np.pad(table, ((0, 0), (0, 256 - columns))))
        at += rows
    return np.concatenate(packed), places


def exchange_rounds(bunches, pencils):
    if bunches == 8 and pencils == 2 and SPAN == 3:
        cycles = (((0, 1, 3, 5, 7, 6, 4, 2),), ((0, 3, 2), (7, 4, 5)), ((1, 2, 5, 6, 3, 4),))
        rounds = []
        for round_cycles in cycles:
            seen = [0] * bunches
            pairs = []
            for cycle in round_cycles:
                for start, end in zip(cycle, cycle[1:] + cycle[:1]):
                    pairs.append((start * 2 + seen[start], end * 2 + seen[end]))
                    seen[start] += 1
                    seen[end] += 1
            pairs += [(2 * bunch, 2 * bunch + 1) for bunch in range(bunches) if not seen[bunch]]
            rounds.append(pairs)
        return rounds
    return [
        [(bunch * pencils, (bunch - distance) * pencils + 1) for bunch in range(distance, bunches)]
        for distance in range(SPAN, 0, -1)
    ]


def round_offsets(rounds, bunches, pencils):
    met = [{bunch} for bunch in range(bunches)]
    tables = []
    for pairs in rounds:
        offsets = [0] * (bunches * pencils)
        counts = [0] * (bunches * pencils)
        for pair in pairs:
            for here, there in (pair, pair[::-1]):
                bunch, source = here // pencils, there // pencils
                if abs(bunch - source) <= SPAN and source not in met[bunch]:
                    met[bunch].add(source)
                    offsets[here] = bunch - source
                    counts[here] = 1
        tables.append((offsets, counts))
    for bunch in range(bunches):
        assert met[bunch] == {b for b in range(bunches) if abs(b - bunch) <= SPAN}
    return tables


def lookup(values, index):
    found = jnp.int32(values[0])
    for at, value in enumerate(values):
        if value != values[0]:
            found = jnp.where(index == at, jnp.int32(value), found)
    return found


def in_hbm(array):
    return pltpu.with_memory_space_constraint(array, pltpu.HBM)


def in_vmem(array):
    return pltpu.with_memory_space_constraint(array, pltpu.VMEM)


def dot(a, b):
    return jnp.dot(a, b, preferred_element_type=F32)


def split(value):
    top = value.astype(BF16)
    return top, (value - top.astype(F32)).astype(BF16)


def data_terms(value):
    top, rest = split(value)
    return jnp.concatenate([top, rest, top], axis=0)


def one_hot(index, rows, value):
    place = lax.broadcasted_iota(jnp.int16, (rows, index.shape[1]), 0)
    return jnp.where(place == index.astype(jnp.int16), value, jnp.zeros((), BF16))


def two_term_dot(table, value):
    out = dot(table, jnp.concatenate(split(value), axis=0))
    half = out.shape[0] // 2
    return out[:half] + out[half:]


def deposit_kernel(particles_ref, table_hbm, out_ref, table_ref, arrived):
    copy = pltpu.make_async_copy(table_hbm, table_ref, arrived)
    copy.start()
    particles = particles_ref[...]
    cell = particles >> CHARGE_BITS
    charge = (particles & (2**CHARGE_BITS - 1)).astype(F32) * (1.0 / CHARGE_UNITS)
    row = ((cell >> 6) & 31) * 8 + (cell >> 13)
    column = ((cell >> 11) & 3) * 64 + (cell & 63)
    out_ref[...] = lax.dot_general(
        one_hot(row, 256, jnp.ones((), BF16)),
        one_hot(column, 256, charge.astype(BF16)),
        (((1,), (1,)), ((), ())),
        preferred_element_type=F32,
    )
    copy.wait()


def deposit(cells, charge, packed):
    units = (charge.astype(F32) * CHARGE_UNITS).astype(jnp.int32)
    particles = (cells << CHARGE_BITS) + units
    return pl.pallas_call(
        deposit_kernel,
        in_specs=[
            pl.BlockSpec(memory_space=pltpu.VMEM),
            pl.BlockSpec(memory_space=pltpu.HBM),
        ],
        out_specs=[pl.BlockSpec(memory_space=pltpu.VMEM)] * 2,
        out_shape=[
            jax.ShapeDtypeStruct((256, 256), F32),
            jax.ShapeDtypeStruct(packed.shape, packed.dtype),
        ],
        scratch_shapes=[pltpu.SemaphoreType.DMA],
        compiler_params=pltpu.CompilerParams(vmem_limit_bytes=VMEM_LIMIT),
        name="deposit",
    )(in_vmem(particles), in_hbm(jnp.asarray(packed)))


def table_rows(table_ref, places, name, pencil=None):
    start, rows, columns = places[name]
    if pencil is not None:
        start = pl.multiple_of(start + pencil * rows, 16)
    return table_ref[pl.ds(start, rows), :columns]


def stage_zx(density, table_z, table_x, after_z, after_x, at):
    top, rest = split(density)
    for low in range(4):
        lanes = slice(low * GZ, (low + 1) * GZ)
        terms = jnp.concatenate([top[:, lanes], rest[:, lanes], top[:, lanes]], axis=1)
        after_z[:, 2 * MZ * low : 2 * MZ * (low + 1)] = dot(terms, table_z)
    for group in range(GY // 4):
        sides = []
        for y in range(4 * group, 4 * group + 4):
            tiles = [
                after_z[8 * y : 8 * y + 8, (2 * low + part) * MZ : (2 * low + part + 1) * MZ]
                for part in range(2)
                for low in range(4)
            ]
            sides.append(jnp.concatenate(tiles, axis=0))
        out = dot(table_x, data_terms(jnp.concatenate(sides, axis=1)))
        for side in range(4):
            rows = pl.ds((4 * group + side) * PITCH_X, 2 * MX)
            after_x[at, rows, :] = out[:, side * MZ : (side + 1) * MZ]


def spectral_kernel(places, offsets, first, last, *refs):
    refs = list(refs)
    count = len(offsets)
    densities = [refs.pop(0) for _ in range(count)]
    green_ref = refs.pop(0)
    table_ref = refs.pop(0)
    before_ref = None if first else refs.pop(0)
    out_ref = refs.pop(0)
    after_z = refs.pop(0)
    after_x = refs.pop(0)
    green = refs.pop(0)
    arrived = refs.pop(0)
    total, back = (refs.pop(0), refs.pop(0)) if last else (out_ref, None)
    width = green_ref.shape[3]
    block = KX_BLOCK
    pencil = lax.axis_index("pencil")
    device = lax.axis_index("bunch") * lax.axis_size("pencil") + pencil
    chosen = [SPAN + lookup(values, device) for values, _ in offsets]

    def copy(at, step):
        kx = pl.ds(step * block, block)
        return pltpu.make_async_copy(
            green_ref.at[chosen[at], :, kx], green.at[at, :, kx], arrived.at[at, step]
        )

    for step in range(MX // block):
        for at in range(count):
            copy(at, step).start()

    def table(name):
        return table_rows(table_ref, places, name, pencil if name in ("y", "iy") else None)

    for at, density_ref in enumerate(densities):
        density = density_ref[...]
        if min(offsets[at][1]) == 0:
            density = density * lookup(offsets[at][1], device).astype(F32)
        stage_zx(density, table("z"), table("x"), after_z, after_x, at)

    def kx_block(step):
        for at in range(count):
            copy(at, step).wait()
        for pair in range(block // 2):
            sums = [[None, None], [None, None]]
            starts = [
                pl.multiple_of((step * block + 2 * pair + side) * width, width) for side in range(2)
            ]
            if not first:
                for side in range(2):
                    rows = pl.ds(starts[side], width)
                    sums[side] = [before_ref[rows, :MZ], before_ref[rows, MZ:]]
            for at in range(count):
                sides = []
                for side in range(2):
                    kx = step * block + 2 * pair + side
                    real = after_x[at, pl.ds(kx, GY, stride=PITCH_X), :]
                    imag = after_x[at, pl.ds(MX + kx, GY, stride=PITCH_X), :]
                    sides.append(jnp.concatenate([real, imag], axis=0))
                out = two_term_dot(table("y"), jnp.concatenate(sides, axis=1))
                for side in range(2):
                    kx = step * block + 2 * pair + side
                    real = out[:width, side * MZ : (side + 1) * MZ]
                    imag = out[width:, side * MZ : (side + 1) * MZ]
                    green_real = green[at, 0, kx]
                    green_imag = green[at, 1, kx]
                    terms = (
                        green_real * real - green_imag * imag,
                        green_real * imag + green_imag * real,
                    )
                    for part in range(2):
                        held = sums[side][part]
                        sums[side][part] = terms[part] if held is None else held + terms[part]
            for side in range(2):
                rows = pl.ds(starts[side], width)
                total[rows, :MZ] = sums[side][0]
                total[rows, MZ:] = sums[side][1]

    pl.loop(0, MX // block)(kx_block)
    if not last:
        return

    lane = lax.broadcasted_iota(jnp.int32, (GY, 2 * GZ), 1)
    front = lane < GZ

    lane = lax.broadcasted_iota(jnp.int32, (GY, 2 * GZ), 1)
    front = lane < GZ
    def back_block(step):
        start = pl.multiple_of(step * block * width, block * width)
        top, rest = split(total[pl.ds(start, block * width), :])
        both = table("iz")
        wide = dot(top, both)
        turned = wide[:, : 2 * GZ] + (wide[:, 2 * GZ :] + dot(rest, both[:, : 2 * GZ]))
        for pair in range(block // 2):
            sides = [
                turned[(2 * pair + side) * width : (2 * pair + side + 1) * width, :]
                for side in range(2)
            ]
            out = dot(table("iy"), data_terms(jnp.concatenate(sides, axis=1)))
            for side in range(2):
                kx = step * block + 2 * pair + side
                by_cos = out[:GY, side * 2 * GZ : (side + 1) * 2 * GZ]
                by_sin = pltpu.roll(out[GY:, side * 2 * GZ : (side + 1) * 2 * GZ], GZ, 1)
                back[pl.ds(kx * PITCH_Y, GY), :] = by_cos + jnp.where(front, -by_sin, by_sin)

    pl.loop(0, MX // block)(back_block)
    for pair in range(GY // 2):
        sides = [back[pl.ds(2 * pair + side, MX, stride=PITCH_Y), :] for side in range(2)]
        out = dot(table("ix"), data_terms(jnp.concatenate(sides, axis=1)))
        even = out[:GX, : 2 * GZ] - pltpu.roll(out[GX:, : 2 * GZ], GZ, 1)
        odd = pltpu.roll(out[:GX, 2 * GZ :], GZ, 1) - out[GX:, 2 * GZ :]
        out_ref[pair * GX : (pair + 1) * GX, :] = jnp.where(front, even, odd)


def spectral(offsets, densities, green, tables, before, last):
    count = len(densities)
    first = before is None
    width = green.shape[3]
    packed, places = tables
    scratch = [
        pltpu.VMEM((256, 1024), F32),
        pltpu.VMEM((count, GY * PITCH_X, MZ), F32),
        pltpu.VMEM((count,) + green.shape[1:], F32),
        pltpu.SemaphoreType.DMA((count, MX // KX_BLOCK)),
    ]
    out_shape = jax.ShapeDtypeStruct((MX * width, 2 * MZ), F32)
    if last:
        scratch.append(pltpu.VMEM((MX * width, 2 * MZ), F32))
        scratch.append(pltpu.VMEM((MX * PITCH_Y, 2 * GZ), F32))
        out_shape = jax.ShapeDtypeStruct((512, 128), F32)
    vmem = pl.BlockSpec(memory_space=pltpu.VMEM)
    return pl.pallas_call(
        functools.partial(spectral_kernel, places, offsets, first, last),
        in_specs=[
            *([vmem] * count),
            pl.BlockSpec(memory_space=pltpu.HBM),
            vmem,
            *([] if first else [vmem]),
        ],
        out_specs=vmem,
        scratch_shapes=scratch,
        out_shape=out_shape,
        compiler_params=pltpu.CompilerParams(vmem_limit_bytes=VMEM_LIMIT),
        cost_estimate=pl.CostEstimate(
            flops=2 * count * STAGE_FLOPS, bytes_accessed=count * 2**21, transcendentals=0
        ),
        name="spectral_last" if last else "spectral_part",
    )(
        *map(in_vmem, densities),
        in_hbm(green),
        in_vmem(packed),
        *([] if first else [in_vmem(before)]),
    )


def gather_kernel(own_ref, other_ref, cell_ref, out_ref, field):
    potential = own_ref[...] + other_ref[...]
    lane = lax.broadcasted_iota(jnp.int32, (512, 128), 1)
    row = lax.broadcasted_iota(jnp.int32, (512, 128), 0)
    x = row % GX
    z = lane % GZ
    zero = jnp.zeros((GX, 128), F32)
    below = jnp.where(x == 0, 0.0, pltpu.roll(potential, 1, 0))
    above = jnp.where(x == GX - 1, 0.0, pltpu.roll(potential, 511, 0))
    field_x = 0.5 * (below - above)
    turned = pltpu.roll(potential, GZ, 1)
    before = jnp.concatenate([zero, turned[: 512 - GX]], axis=0)
    after = jnp.concatenate([turned[GX:], zero], axis=0)
    field_y = 0.5 * (
        jnp.where(lane < GZ, before, turned) - jnp.where(lane < GZ, turned, after)
    )
    left = jnp.where(z == 0, 0.0, pltpu.roll(potential, 1, 1))
    right = jnp.where(z == GZ - 1, 0.0, pltpu.roll(potential, 127, 1))
    field_z = 0.5 * (left - right)
    for part, value in enumerate((field_x, field_y, field_z)):
        field[part * 128 : (part + 1) * 128, :] = jnp.transpose(value).astype(BF16)

    count = cell_ref.shape[1]
    chunk = min(GATHER_CHUNK, count)
    for at in range(0, count, chunk):
        cell = cell_ref[:, at : at + chunk]
        y = (cell >> 6) & 31
        high = (y >> 1) * GX + (cell >> 11)
        low = (y & 1) * GZ + (cell & 63)
        picked = dot(field[...], one_hot(high, 512, jnp.ones((), BF16)))
        inside = lax.broadcasted_iota(jnp.int32, (128, chunk), 0) == low
        for part in range(3):
            values = jnp.where(inside, picked[part * 128 : (part + 1) * 128], 0.0)
            out_ref[part, :, at : at + chunk] = jnp.sum(values, axis=0, keepdims=True)


def gather(own, other, cells):
    return pl.pallas_call(
        gather_kernel,
        out_shape=jax.ShapeDtypeStruct((3, 1, cells.shape[1]), F32),
        scratch_shapes=[pltpu.VMEM((384, 512), BF16)],
        compiler_params=pltpu.CompilerParams(vmem_limit_bytes=48 * 2**20),
        name="gather",
    )(own, other, cells)


def per_device(tables, charge, cell_deposit, cell_gather, green_spectra):
    pencils = lax.axis_size("pencil")
    bunches = lax.axis_size("bunch")
    swap = [(i, (i + 1) % pencils) for i in range(pencils)]
    packed, places = tables
    part, packed = deposit(cell_deposit, charge, packed)
    tables = (packed, places)
    particles = charge.shape[1] * pencils
    scale = 2.0 ** (15 - math.ceil(math.log2(particles * MOST_CHARGE)))
    def received(array):
        return array.astype(F32) * (1.0 / scale)

    partial = (part * scale).astype(jnp.float16)
    density = part + received(lax.ppermute(partial, "pencil", swap))
    rounds = exchange_rounds(bunches, pencils)
    offsets = round_offsets(rounds, bunches, pencils)
    sent = (density * scale).astype(jnp.float16)
    near = []
    for pairs in rounds:
        route = [*pairs, *(pair[::-1] for pair in pairs)]
        near.append(lax.ppermute(sent, ("bunch", "pencil"), route))

    def terms(offsets, densities, before, last):
        return spectral(offsets, densities, green_spectra, tables, before, last)

    devices = bunches * pencils
    total = terms([([0] * devices, [1] * devices)], [density], None, False)
    far = []
    for group in NEAR_GROUPS:
        arrivals = [near[at] for at in group]
        total, arrivals = lax.optimization_barrier((total, arrivals))
        beyond = lax.ppermute(jnp.concatenate(arrivals), "pencil", swap)
        far += jnp.split(beyond, len(group))
        arrivals = [received(each) for each in arrivals]
        total = terms([offsets[at] for at in group], arrivals, total, False)

    def beside(values):
        return [values[bunch * pencils + (core + 1) % pencils] for bunch in range(bunches) for core in range(pencils)]

    far_offsets = [tuple(map(beside, offsets[at])) for group in NEAR_GROUPS for at in group]
    own = terms(far_offsets, [received(each) for each in far], total, True)
    other = lax.ppermute(own, "pencil", swap)
    return gather(own, other, cell_gather)


def solution(mesh):
    in_specs = (
        P(("groups", "bunch"), "pencil"),
        P(("groups", "bunch"), "pencil"),
        P(("groups", "bunch"), "pencil"),
        P(None, None, None, "pencil", None),
    )
    out_specs = P(None, ("groups", "bunch"), "pencil")
    tables = make_tables(mesh.shape["pencil"])
    return jax.shard_map(
        functools.partial(per_device, tables),
        mesh=mesh,
        in_specs=in_specs,
        out_specs=out_specs,
        check_vma=False,
    )
```
